32 devices in a mesh: parts: 2 (over y), tensor: 4 (over z), dp: 4 (over x, core).
Axes of the slice: x: 2, y: 2, z: 4, core: 2. Of those that a mesh axis runs over, the one named last changes fastest.
Arguments:
- layer_input_states: bfloat16 [4, 128, 5120], P(None, ('parts', 'dp'), 'tensor'), parts along dimension 1, may hold values from -80 to 80
- base_query_weight: bfloat16 [5120, 4096], P(None, 'tensor'), may hold values from -0.078125 to 0.078125
- key_value_weight: bfloat16 [5120, 1024], P('tensor'), may hold values from -0.078125 to 0.078125
- output_weight: bfloat16 [4096, 5120], P('tensor'), may hold values from -0.09375 to 0.09375
- stored_keys: bfloat16 [4, 128, 128, 128], P(None, ('parts', 'dp'), 'tensor'), parts along dimension 1, may hold values from -300 to 300
- stored_values: bfloat16 [4, 128, 128, 128], P(None, ('parts', 'dp'), 'tensor'), parts along dimension 1, may hold values from -6 to 6
- lengths: int32 [128], P(('parts', 'dp')), parts along dimension 0, may hold values from 4 to 124, as said below
- adapter_down: float32 [64, 10240], P(None, ('parts', 'tensor')), parts along dimension 1, may hold values from -0.078125 to 0.078125
- down_first_moment: float32 [64, 10240], P(None, ('parts', 'tensor')), parts along dimension 1, may hold values from -6 to 6
- down_second_moment: float32 [64, 10240], P(None, ('parts', 'tensor')), parts along dimension 1, may hold values from 0.5 to 20
- down_gradients: float32 [4, 64, 10240], P('dp', None, ('parts', 'tensor')), parts along dimension 2, may hold values from -6 to 6
- adapter_up: float32 [64, 8192], P(None, ('parts', 'tensor')), parts along dimension 1, may hold values from -0.375 to 0.375
- up_first_moment: float32 [64, 8192], P(None, ('parts', 'tensor')), parts along dimension 1, may hold values from -6 to 6
- up_second_moment: float32 [64, 8192], P(None, ('parts', 'tensor')), parts along dimension 1, may hold values from 0.5 to 20
- up_gradients: float32 [4, 64, 8192], P('dp', None, ('parts', 'tensor')), parts along dimension 2, may hold values from -6 to 6
Outputs:
- adapter_down_next: float32 [64, 10240], P(None, ('parts', 'tensor')), parts along dimension 1
- down_first_moment_next: float32 [64, 10240], P(None, ('parts', 'tensor')), parts along dimension 1
- down_second_moment_next: float32 [64, 10240], P(None, ('parts', 'tensor')), parts along dimension 1
- adapter_up_next: float32 [64, 8192], P(None, ('parts', 'tensor')), parts along dimension 1
- up_first_moment_next: float32 [64, 8192], P(None, ('parts', 'tensor')), parts along dimension 1
- up_second_moment_next: float32 [64, 8192], P(None, ('parts', 'tensor')), parts along dimension 1
- layer_out: bfloat16 [4, 128, 5120], P(None, ('parts', 'dp'), 'tensor'), parts along dimension 1
The draws below stay inside these ranges and needn't reach their ends.
There are 2 independent parts, one for each index of `parts`. The reference program is written for one: setup_inputs(seed, part) draws one part's arguments, and reference() takes and returns one part's arrays. A program takes and returns all parts, laid end to end along the dimension named above; an argument that names none is the same for every part. Nothing has to cross between parts.
Inputs may be any that keep to these rules, and one draw needn't show every extreme that they name: `lengths`: the longest row reaches 124.
All inputs are finite; a program needn't handle non-finite values.
Results may differ from the reference program's by a relative error of at most 0.012.
The reference program's roundings to bfloat16 on the way count: a program that leaves them out, or rounds other values in their place, can miss the bound.
Values may be sent and summed in bfloat16 or wider, within the bound.
A program may use at most 128 MiB of HBM per device.

```python
import math
import jax
import jax.numpy as jnp
from jax import lax

MODEL_WIDTH = 5120
QUERY_HEAD_COUNT = 32
KEY_VALUE_HEADS = 4
HEAD_SIZE = 128
ADAPTER_RANK = 64
DECODE_STEPS = 4
QUERY_WIDTH = 4096
KVW = 1024
TOTAL_ROWS = 64
CACHE_LENGTH = 128
REPLICAS = 4


def draw_layer_input_states(key, part):
    key = jax.random.fold_in(key, 11)
    first, second_moment, third = jax.random.split(key, 3)
    array_shape = (DECODE_STEPS, TOTAL_ROWS, MODEL_WIDTH)
    row_scale = 10.0 ** jax.random.uniform(second_moment, (DECODE_STEPS, TOTAL_ROWS, 1), minval=-0.3, maxval=0.7)
    col_scale = 10.0 ** jax.random.uniform(third, (1, 1, MODEL_WIDTH), minval=-0.5, maxval=0.5)
    base = jnp.clip(jax.random.normal(first, array_shape), -4.0, 4.0)
    return (base * row_scale * col_scale).astype(jnp.bfloat16)


def draw_stored_keys(key, part):
    key = jax.random.fold_in(key, 23)
    first = jax.random.fold_in(key, 0)
    array_shape = (KEY_VALUE_HEADS, TOTAL_ROWS, CACHE_LENGTH, HEAD_SIZE)
    base = jnp.clip(jax.random.normal(first, array_shape), -4.0, 4.0)
    return base.astype(jnp.bfloat16)


def draw_lengths(key, part):
    key = jax.random.fold_in(key, 37)
    drawn = jax.random.randint(key, (TOTAL_ROWS,), 4, CACHE_LENGTH - DECODE_STEPS + 1)
    return drawn.at[0].set(CACHE_LENGTH - DECODE_STEPS).astype(jnp.int32)


def level_of(stream_key, shape, cuts, least, high):
    def one(axis_at, blocks):
        heights = jax.random.uniform(jax.random.fold_in(jax.random.fold_in(stream_key, 6), axis_at), (blocks,), jnp.float32, least / len(cuts), high / len(cuts))
        return jnp.repeat(jnp.exp(heights), shape[axis_at] // blocks).reshape((-1,) + (1,) * (len(shape) - axis_at - 1))

    loudness = one(*cuts[0])
    for cut in cuts[1:]:
        loudness = loudness * one(*cut)
    return loudness


def bell_draw(key, shape, scale, most, cuts=(), kind=jnp.bfloat16):
    result = jax.random.normal(key, shape, jnp.float32) * scale
    if len(cuts) > 0:
        result = level_of(key, shape, cuts, -0.22, 0.18) * result
    return jnp.clip(result, min=-most, max=most).astype(kind)


def setup_inputs(seed: int = 0, part: int = 0) -> dict:
    streams_of = jax.random.split(jax.random.key(seed), 16)
    own_keys = jax.random.split(jax.random.fold_in(streams_of[15], part), 16)
    return {
        "layer_input_states": draw_layer_input_states(jax.random.fold_in(jax.random.fold_in(streams_of[15], part), 71), part),
        "base_query_weight": bell_draw(streams_of[1], (MODEL_WIDTH, QUERY_WIDTH), MODEL_WIDTH ** -0.5, 0.078125, ((1, 4),)),
        "key_value_weight": bell_draw(streams_of[2], (MODEL_WIDTH, KVW), MODEL_WIDTH ** -0.5, 0.078125, ((0, 4),)),
        "output_weight": bell_draw(streams_of[3], (QUERY_WIDTH, MODEL_WIDTH), QUERY_WIDTH ** -0.5, 0.09375, ((0, 4),)),
        "stored_keys": draw_stored_keys(jax.random.fold_in(jax.random.fold_in(streams_of[15], part), 71), part),
        "stored_values": bell_draw(own_keys[5], (KEY_VALUE_HEADS, TOTAL_ROWS, CACHE_LENGTH, HEAD_SIZE), 1.0, 6.0, ((1, 4), (2, 4))),
        "lengths": draw_lengths(jax.random.fold_in(jax.random.fold_in(streams_of[15], part), 71), part),
        "adapter_down": bell_draw(own_keys[7], (ADAPTER_RANK, MODEL_WIDTH), MODEL_WIDTH ** -0.5, 0.078125, ((1, 4),), jnp.float32),
        "down_first_moment": bell_draw(own_keys[8], (ADAPTER_RANK, MODEL_WIDTH), 1.0, 6.0, ((1, 4),), jnp.float32),
        "down_second_moment": jnp.clip(jnp.exp(math.log(20.0) - 3.6888795 * jax.random.uniform(own_keys[9], (ADAPTER_RANK, MODEL_WIDTH), jnp.float32) ** level_of(own_keys[9], (ADAPTER_RANK, MODEL_WIDTH), ((1, 4),), -0.2, 0.2)), 0.5, 20.0),
        "down_gradients": bell_draw(own_keys[10], (REPLICAS, ADAPTER_RANK, MODEL_WIDTH), 1.0, 6.0, ((0, 4), (2, 4)), jnp.float32),
        "adapter_up": bell_draw(own_keys[11], (ADAPTER_RANK, QUERY_WIDTH), (4 * ADAPTER_RANK) ** -0.5, 0.375, ((1, 4),), jnp.float32),
        "up_first_moment": bell_draw(own_keys[12], (ADAPTER_RANK, QUERY_WIDTH), 1.0, 6.0, ((1, 4),), jnp.float32),
        "up_second_moment": jnp.clip(jnp.exp(math.log(20.0) - 3.6888795 * jax.random.uniform(own_keys[13], (ADAPTER_RANK, QUERY_WIDTH), jnp.float32) ** level_of(own_keys[13], (ADAPTER_RANK, QUERY_WIDTH), ((1, 4),), -0.2, 0.2)), 0.5, 20.0),
        "up_gradients": bell_draw(own_keys[14], (REPLICAS, ADAPTER_RANK, QUERY_WIDTH), 1.0, 6.0, ((0, 4), (2, 4)), jnp.float32),
    }


beta_one = 0.9
beta_two = 0.999
learn_rate = 0.01
adam_eps = 1e-08
bias_one = 1.0 - (0.9 ** 50) ** 2
bias_two = 1.0 - (0.999 ** 50) ** 2
adapter_scale = 2.0
norm_eps = 1e-06

def moment_optimizer_update(param, moment, second_moment, grad):
    moment_new = beta_one * moment + (1.0 - beta_one) * grad
    second_new = beta_two * second_moment + (1.0 - beta_two) * grad * grad
    step_size = moment_new / bias_one / (jnp.sqrt(second_new / bias_two) + adam_eps)
    return (param - learn_rate * step_size, moment_new, second_new)

def reference(layer_input_states, base_query_weight, key_value_weight, output_weight, stored_keys, stored_values, lengths, adapter_down, down_first_moment, down_second_moment, down_gradients, adapter_up, up_first_moment, up_second_moment, up_gradients):
    adapter_down_next, down_first_moment_next, down_second_moment_next = moment_optimizer_update(adapter_down, down_first_moment, down_second_moment, lax.optimization_barrier(jnp.sum(down_gradients, axis=0)))
    adapter_up_next, up_first_moment_next, up_second_moment_next = moment_optimizer_update(adapter_up, up_first_moment, up_second_moment, lax.optimization_barrier(jnp.sum(up_gradients, axis=0)))
    factor_update = jnp.dot(adapter_down_next.T, adapter_up_next, precision=lax.Precision.HIGHEST, preferred_element_type=jnp.float32)
    merged_query_weight = (base_query_weight.astype(jnp.float32) + adapter_scale * factor_update).astype(jnp.bfloat16)
    widened = layer_input_states.astype(jnp.float32)
    inverse = lax.rsqrt(lax.optimization_barrier(jnp.mean(widened * widened, axis=-1, keepdims=True)) + norm_eps)
    flattened = (widened * inverse).astype(jnp.bfloat16).reshape(DECODE_STEPS * TOTAL_ROWS, MODEL_WIDTH)
    query_rows = jnp.dot(flattened, merged_query_weight, preferred_element_type=jnp.float32).astype(jnp.bfloat16)
    query_rows = query_rows.reshape(DECODE_STEPS, TOTAL_ROWS, KEY_VALUE_HEADS, QUERY_HEAD_COUNT // KEY_VALUE_HEADS, HEAD_SIZE).astype(jnp.float32)
    key_value_rows = jnp.dot(flattened, key_value_weight, preferred_element_type=jnp.float32).astype(jnp.bfloat16)
    key_value_rows = key_value_rows.reshape(DECODE_STEPS, TOTAL_ROWS, 2, KEY_VALUE_HEADS, HEAD_SIZE)
    slot_index = jnp.arange(CACHE_LENGTH, dtype=jnp.int32)
    key_cache = stored_keys
    value_cache = stored_values
    for step_index in range(DECODE_STEPS):
        written = (slot_index[None, :] == lengths[:, None] + step_index)[None, :, :, None]
        new_keys = jnp.transpose(key_value_rows[step_index, :, 0], (1, 0, 2))[:, :, None, :]
        new_values = jnp.transpose(key_value_rows[step_index, :, 1], (1, 0, 2))[:, :, None, :]
        key_cache = jnp.where(written, new_keys, key_cache)
        value_cache = jnp.where(written, new_values, value_cache)
    key_wide = key_cache.astype(jnp.float32)
    value_wide = value_cache.astype(jnp.float32)
    outputs = []
    for step_index in range(DECODE_STEPS):
        visible = slot_index[None, :] < lengths[:, None] + step_index + 1
        scores = jnp.einsum('rhgd,hrcd->hgrc', query_rows[step_index], key_wide) * HEAD_SIZE ** (-0.5)
        scores = jnp.where(visible[None, None], scores, -1e+30)
        row_max = lax.optimization_barrier(jnp.max(scores, axis=-1, keepdims=True))
        weights = jnp.where(visible[None, None], jnp.exp(scores - row_max), 0.0)
        totals = lax.optimization_barrier(jnp.sum(weights, axis=-1))
        rounded = weights.astype(jnp.bfloat16).astype(jnp.float32)
        blended = jnp.einsum('hgrc,hrcd->hgrd', rounded, value_wide) / totals[..., None]
        attended = jnp.transpose(blended, (2, 0, 1, 3)).reshape(TOTAL_ROWS, QUERY_WIDTH).astype(jnp.bfloat16)
        outputs.append(jnp.dot(attended, output_weight, preferred_element_type=jnp.float32).astype(jnp.bfloat16))
    layer_out = jnp.stack(outputs)
    return (adapter_down_next, down_first_moment_next, down_second_moment_next, adapter_up_next, up_first_moment_next, up_second_moment_next, layer_out)
```

```python
import functools

import jax
import jax.numpy as jnp
from jax import lax
from jax.experimental import pallas as pl
from jax.experimental.pallas import tpu as pltpu
from jax.sharding import PartitionSpec as P

QUERY_HEAD_COUNT = 32
KEY_VALUE_HEADS = 4
HEAD_SIZE = 128


beta_one = 0.9
beta_two = 0.999
learn_rate = 0.01
adam_eps = 1e-08
bias_one = 1.0 - (0.9**50) ** 2
bias_two = 1.0 - (0.999**50) ** 2
adapter_scale = 2.0
norm_eps = 1e-06


def moment_optimizer_update(param, moment, second_moment, grad):
    moment_new = beta_one * moment + (1.0 - beta_one) * grad
    second_new = beta_two * second_moment + (1.0 - beta_two) * grad * grad
    step_size = moment_new / bias_one / (jnp.sqrt(second_new / bias_two) + adam_eps)
    return (param - learn_rate * step_size, moment_new, second_new)


def general_shards(
    layer_input_states,
    base_query_weight,
    key_value_weight,
    output_weight,
    stored_keys,
    stored_values,
    lengths,
    adapter_down,
    down_first_moment,
    down_second_moment,
    down_gradients,
    adapter_up,
    up_first_moment,
    up_second_moment,
    up_gradients,
):
    tensor_count = lax.axis_size("tensor")
    tensor_rank = lax.axis_index("tensor")
    summed_down_gradient, summed_up_gradient = lax.psum((down_gradients[0], up_gradients[0]), "dp")
    adapter_down_next, down_first_moment_next, down_second_moment_next = moment_optimizer_update(
        adapter_down, down_first_moment, down_second_moment, summed_down_gradient
    )
    adapter_up_next, up_first_moment_next, up_second_moment_next = moment_optimizer_update(
        adapter_up, up_first_moment, up_second_moment, summed_up_gradient
    )
    plain_query_rows = base_query_weight.astype(jnp.float32)
    factor_update = lax.dot_general(
        lax.all_gather(adapter_down_next, "tensor", axis=1, tiled=True),
        adapter_up_next,
        (((0,), (0,)), ((), ())),
        precision=lax.Precision.HIGHEST,
        preferred_element_type=jnp.float32,
    )
    merged_query_weight = (plain_query_rows + adapter_scale * factor_update).astype(jnp.bfloat16)
    heads_local = QUERY_HEAD_COUNT // tensor_count
    local_ctx = stored_keys.shape[2]
    slot_index = tensor_rank * local_ctx + jnp.arange(local_ctx, dtype=jnp.int32)
    score_scale = HEAD_SIZE ** (-0.5)
    key_cache = stored_keys
    value_cache = stored_values
    pieces = []
    for step_index in range(layer_input_states.shape[0]):
        hidden_block = layer_input_states[step_index : step_index + 1]
        decode_key_cache = key_cache
        decode_value_cache = value_cache
        optimizer_step_count = hidden_block.shape[0]
        decode_row_count = hidden_block.shape[1]
        gathered = lax.all_gather(hidden_block, "tensor", axis=2, tiled=True)
        widened = gathered.astype(jnp.float32)
        inverse = lax.rsqrt(jnp.mean(widened * widened, axis=-1, keepdims=True) + norm_eps)
        normed = (widened * inverse).astype(jnp.bfloat16)
        normed_local = (hidden_block.astype(jnp.float32) * inverse).astype(jnp.bfloat16)
        partial_kv = jnp.einsum(
            "srd,de->sre", normed_local, key_value_weight, preferred_element_type=jnp.float32
        )
        key_value_rows = lax.psum(partial_kv, "tensor").astype(jnp.bfloat16)
        key_value_rows = key_value_rows.reshape(
            optimizer_step_count, decode_row_count, 2, KEY_VALUE_HEADS, HEAD_SIZE
        )
        queries_local = jnp.einsum(
            "srd,de->sre", normed, merged_query_weight, preferred_element_type=jnp.float32
        ).astype(jnp.bfloat16)
        query_rows = lax.all_gather(queries_local, "tensor", axis=2, tiled=True)
        query_rows = query_rows.reshape(
            optimizer_step_count,
            decode_row_count,
            KEY_VALUE_HEADS,
            QUERY_HEAD_COUNT // KEY_VALUE_HEADS,
            HEAD_SIZE,
        )
        written = (slot_index[None, :] == lengths[:, None] + step_index + 0)[None, :, :, None]
        new_keys = jnp.transpose(key_value_rows[0, :, 0], (1, 0, 2))[:, :, None, :]
        new_values = jnp.transpose(key_value_rows[0, :, 1], (1, 0, 2))[:, :, None, :]
        decode_key_cache = jnp.where(written, new_keys, decode_key_cache)
        decode_value_cache = jnp.where(written, new_values, decode_value_cache)
        step_offsets = step_index + 1 + jnp.arange(optimizer_step_count, dtype=jnp.int32)
        visible = slot_index[None, None, :] < lengths[None, :, None] + step_offsets[:, None, None]
        visible = visible[:, None, None, :, :]
        scores = (
            jnp.einsum(
                "srhgd,hrcd->shgrc",
                query_rows,
                decode_key_cache,
                preferred_element_type=jnp.float32,
            )
            * score_scale
        )
        scores = jnp.where(visible, scores, -1e30)
        row_max = jnp.max(scores, axis=-1)
        weights = jnp.where(visible, jnp.exp(scores - row_max[..., None]), 0.0)
        totals = jnp.sum(weights, axis=-1)
        blended = jnp.einsum(
            "shgrc,hrcd->shgrd",
            weights.astype(jnp.bfloat16),
            decode_value_cache,
            preferred_element_type=jnp.float32,
        )
        blended = blended.reshape(
            optimizer_step_count, tensor_count, heads_local, decode_row_count, HEAD_SIZE
        )
        row_max = row_max.reshape(optimizer_step_count, tensor_count, heads_local, decode_row_count)
        totals = totals.reshape(optimizer_step_count, tensor_count, heads_local, decode_row_count)
        blended_in = lax.all_to_all(blended, "tensor", split_axis=1, concat_axis=1, tiled=True)
        peak_scores = lax.all_to_all(row_max, "tensor", split_axis=1, concat_axis=1, tiled=True)
        masses = lax.all_to_all(totals, "tensor", split_axis=1, concat_axis=1, tiled=True)
        overall = jnp.max(peak_scores, axis=1, keepdims=True)
        factor = jnp.exp(peak_scores - overall)
        denominator = jnp.sum(factor * masses, axis=1)
        combined = jnp.sum(factor[..., None] * blended_in, axis=1) / denominator[..., None]
        combined = jnp.transpose(combined, (0, 2, 1, 3))
        attended = combined.reshape(
            combined.shape[0], combined.shape[1], heads_local * HEAD_SIZE
        ).astype(jnp.bfloat16)
        projected = jnp.einsum(
            "sre,ed->srd", attended, output_weight, preferred_element_type=jnp.float32
        )
        reduced = lax.psum_scatter(projected, "tensor", scatter_dimension=2, tiled=True)
        step_out = reduced.astype(jnp.bfloat16)
        key_cache = decode_key_cache
        value_cache = decode_value_cache
        pieces.append(step_out)
    layer_out = jnp.concatenate(pieces, axis=0)
    return (
        adapter_down_next,
        down_first_moment_next,
        down_second_moment_next,
        adapter_up_next,
        up_first_moment_next,
        up_second_moment_next,
        layer_out,
    )


MESH = pl.DeviceIdType.MESH
F32 = jnp.float32
BF16 = jnp.bfloat16


def split_high_low(value):
    high = value.astype(BF16)
    return high, (value - high.astype(F32)).astype(BF16)


def fused_kernel(
    shards_z,
    x_in,
    base_in,
    kvw_in,
    ow_in,
    keys_in,
    values_in,
    lengths_ref,
    pd_in,
    md_in,
    vd_in,
    gd_in,
    pu_in,
    mu_in,
    vu_in,
    gu_in,
    pd_out,
    md_out,
    vd_out,
    pu_out,
    mu_out,
    vu_out,
    layer_out,
    xg,
    normed,
    base_v,
    kvw_v,
    ow_v,
    keys_v,
    values_v,
    pd,
    md,
    vd,
    pu,
    mu,
    vu,
    gd,
    gu,
    g1d,
    g1u,
    g2d,
    g2u,
    r2d,
    r2u,
    gsd,
    gsu,
    factors,
    up_cat,
    kv_send,
    kv_recv,
    q_acc,
    q_rows,
    blend_rows,
    att,
    out_send,
    out_recv,
    out_final,
    load_sem,
    store_sem,
    z_send,
    z_recv,
    pair_send,
    pair_recv,
):
    t = lax.axis_index("tensor")
    replica = lax.axis_index("dp")
    half = lax.rem(replica, 2)
    other = 1 - half
    mate = replica + 1 - 2 * half
    across = lax.rem(replica + 2, 4)
    rank = pd.shape[0]
    hr = rank // 2
    width = xg.shape[2]
    steps_rows = xg.shape[1]
    mine = pl.ds(pl.multiple_of(half * hr, hr), hr)
    theirs = pl.ds(pl.multiple_of(other * hr, hr), hr)
    peers = [lax.rem(t + d, shards_z) for d in range(1, shards_z)]
    sources = [lax.rem(t + shards_z - d, shards_z) for d in range(1, shards_z)]
    order = range(shards_z - 1)

    def load(index, src, dst):
        copy = pltpu.make_async_copy(src, dst, load_sem.at[index])
        copy.start()
        return copy

    def to_z(kind, d, src, dst):
        copy = pltpu.make_async_remote_copy(
            src_ref=src,
            dst_ref=dst,
            send_sem=z_send.at[kind, d],
            recv_sem=z_recv.at[kind, d],
            device_id={"tensor": peers[d]},
            device_id_type=MESH,
        )
        copy.start()
        return copy

    def to_dp(index, target, src, dst):
        copy = pltpu.make_async_remote_copy(
            src_ref=src,
            dst_ref=dst,
            send_sem=pair_send.at[index],
            recv_sem=pair_recv.at[index],
            device_id={"dp": target},
            device_id_type=MESH,
        )
        copy.start()
        return copy

    barrier = pltpu.get_barrier_semaphore()
    for p in peers:
        pl.semaphore_signal(barrier, inc=1, device_id={"tensor": p}, device_id_type=MESH)
    for p in (mate, across):
        pl.semaphore_signal(barrier, inc=1, device_id={"dp": p}, device_id_type=MESH)
    load_gd = load(0, gd_in, gd)
    load_gu = load(1, gu_in, gu)
    adam_loads = [
        load(2 + i, a, b)
        for i, (a, b) in enumerate(
            ((pd_in, pd), (md_in, md), (vd_in, vd), (pu_in, pu), (mu_in, mu), (vu_in, vu))
        )
    ]
    load_x = load(8, x_in, xg.at[t])
    load_kvw = load(9, kvw_in, kvw_v)
    load_base = load(10, base_in, base_v)
    load_keys = load(11, keys_in.at[t], keys_v.at[t])
    load_values = load(12, values_in.at[t], values_v.at[t])
    load_ow = load(13, ow_in, ow_v)
    pl.semaphore_wait(barrier, shards_z + 1)

    g1 = [
        to_dp(0, mate, gd_in.at[theirs], g1d),
        to_dp(1, mate, gu_in.at[theirs], g1u),
    ]
    sent_x = [to_z(0, d, x_in, xg.at[t]) for d in order]

    load_gd.wait()
    load_gu.wait()
    for copy in g1:
        copy.wait_recv()
    g2d[...] = gd[mine, :] + g1d[...]
    g2u[...] = gu[mine, :] + g1u[...]
    g2 = [to_dp(2, across, g2d, r2d), to_dp(3, across, g2u, r2u)]
    for copy in adam_loads:
        copy.wait()
    for copy in g2:
        copy.wait_recv()
    gsd[mine, :] = g2d[...] + r2d[...]
    gsu[mine, :] = g2u[...] + r2u[...]
    gs = [
        to_dp(4, mate, gsd.at[mine], gsd.at[mine]),
        to_dp(5, mate, gsu.at[mine], gsu.at[mine]),
    ]

    def step_down(rows, which):
        new = moment_optimizer_update(pd[rows, :], md[rows, :], vd[rows, :], gsd[rows, :])
        pd[rows, :], md[rows, :], vd[rows, :] = new
        high, low = split_high_low(new[0])
        factors[t, which, 0:hr, :] = high
        factors[t, which, hr : 2 * hr, :] = low

    step_down(mine, half)
    sent_factors = [to_z(1, d, factors.at[t, half], factors.at[t, half]) for d in order]
    sent_keys = [to_z(3, d, keys_in.at[peers[d]], keys_v.at[t]) for d in order]
    sent_values = [to_z(4, d, values_in.at[peers[d]], values_v.at[t]) for d in order]

    for copy in gs:
        copy.wait_recv()
    step_down(theirs, other)
    new_up = moment_optimizer_update(pu[...], mu[...], vu[...], gsu[...])
    pu[...], mu[...], vu[...] = new_up
    stores = []
    for i, (a, b) in enumerate(
        ((pd, pd_out), (md, md_out), (vd, vd_out), (pu, pu_out), (mu, mu_out), (vu, vu_out))
    ):
        copy = pltpu.make_async_copy(a, b, store_sem.at[i])
        copy.start()
        stores.append(copy)
    up_parts = split_high_low(adapter_scale * new_up[0])
    for i in range(2):
        for j in range(2):
            piece = up_parts[i][j * hr : (j + 1) * hr, :]
            at = (i * 2 + j) * 2 * hr
            up_cat[at : at + hr, :] = piece
            up_cat[at + hr : at + 2 * hr, :] = piece

    load_x.wait()
    for copy in sent_x:
        copy.wait_recv()
    squares = jnp.zeros((steps_rows, 1), F32)
    for b in range(shards_z):
        wide = xg[b].astype(F32)
        squares = squares + jnp.sum(wide * wide, axis=-1, keepdims=True)
    inverse = lax.rsqrt(squares / (width * shards_z) + norm_eps)
    for b in range(shards_z):
        normed[b] = (xg[b].astype(F32) * inverse).astype(BF16)
    load_kvw.wait()
    local_rows = normed[t]
    kv_half = KEY_VALUE_HEADS * HEAD_SIZE
    for p in range(shards_z):
        for kind in range(2):
            at = kind * kv_half + p * HEAD_SIZE
            kv_send[p, :, kind * HEAD_SIZE : (kind + 1) * HEAD_SIZE] = jnp.dot(
                local_rows, kvw_v[:, at : at + HEAD_SIZE], preferred_element_type=F32
            )
    sent_kv = [to_z(2, d, kv_send.at[peers[d]], kv_recv.at[t]) for d in order]

    load_base.wait()
    q_acc[...] = jnp.zeros_like(q_acc)
    tile = 256

    def query_block(b):
        def body(j, carry):
            columns = pl.ds(pl.multiple_of(j * tile, tile), tile)
            left = factors[b, :, :, columns].reshape(2 * rank, tile)
            update = lax.dot_general(
                jnp.concatenate([left, left], axis=0),
                up_cat[...],
                (((0,), (0,)), ((), ())),
                preferred_element_type=F32,
            )
            rows = pl.ds(pl.multiple_of(b * width + j * tile, tile), tile)
            merged = (base_v[rows, :].astype(F32) + update).astype(BF16)
            q_acc[...] += jnp.dot(normed[b, :, columns], merged, preferred_element_type=F32)
            return carry

        lax.fori_loop(0, width // tile, body, 0)

    query_block(t)
    passed = []
    for d in order:
        sent_factors[d].wait_recv()
        slot = factors.at[sources[d], half]
        passed.append(to_dp(6 + d, mate, slot, slot))
    for d in order:
        passed[d].wait_recv()
        query_block(sources[d])

    rows_each = q_rows.shape[0]
    steps = steps_rows // rows_each
    group = q_acc.shape[1] // HEAD_SIZE
    rounded = q_acc[...].astype(BF16).astype(F32)
    for s in range(steps):
        for g in range(group):
            q_rows[:, s * group + g, :] = rounded[
                s * rows_each : (s + 1) * rows_each, g * HEAD_SIZE : (g + 1) * HEAD_SIZE
            ]
    for copy in sent_kv:
        copy.wait_recv()
    new_kv = kv_send[t]
    for d in order:
        new_kv = new_kv + kv_recv[sources[d]]
    new_kv = new_kv.astype(BF16)
    new_keys = new_kv[:, :HEAD_SIZE]
    new_values = new_kv[:, HEAD_SIZE:]
    load_keys.wait()
    load_values.wait()
    for copy in sent_keys + sent_values:
        copy.wait_recv()
    queries = q_rows[...].astype(BF16)
    keys = jnp.concatenate([keys_v[b] for b in range(shards_z)], axis=1)
    values = jnp.concatenate([values_v[b] for b in range(shards_z)], axis=1)
    scale = HEAD_SIZE ** (-0.5)
    pairs = steps * group
    old = (
        lax.dot_general(
            queries, keys, (((2,), (2,)), ((0,), (0,))), preferred_element_type=F32
        )
        * scale
    )
    fresh = (
        lax.dot_general(
            queries.reshape(rows_each * pairs, HEAD_SIZE),
            new_keys,
            (((1,), (1,)), ((), ())),
            preferred_element_type=F32,
        )
        * scale
    ).reshape(rows_each, pairs, steps_rows)
    place = lax.broadcasted_iota(jnp.int32, old.shape, 2)
    seen_old = place < lengths_ref[...]
    column = lax.broadcasted_iota(jnp.int32, fresh.shape, 2)
    row = lax.broadcasted_iota(jnp.int32, fresh.shape, 0)
    step = lax.broadcasted_iota(jnp.int32, fresh.shape, 1) // group
    seen_new = (column % rows_each == row) & (column // rows_each <= step)
    old = jnp.where(seen_old, old, -1e30)
    fresh = jnp.where(seen_new, fresh, -1e30)
    peak = jnp.maximum(
        jnp.max(old, axis=-1, keepdims=True), jnp.max(fresh, axis=-1, keepdims=True)
    )
    old = jnp.where(seen_old, jnp.exp(old - peak), 0.0)
    fresh = jnp.where(seen_new, jnp.exp(fresh - peak), 0.0)
    total = jnp.sum(old, axis=-1, keepdims=True) + jnp.sum(fresh, axis=-1, keepdims=True)
    blended = lax.dot_general(
        old.astype(BF16), values, (((2,), (1,)), ((0,), (0,))), preferred_element_type=F32
    )
    blended = blended + jnp.dot(
        fresh.reshape(rows_each * pairs, steps_rows).astype(BF16),
        new_values,
        preferred_element_type=F32,
    ).reshape(rows_each, pairs, HEAD_SIZE)
    blend_rows[...] = blended / total
    for s in range(steps):
        for g in range(group):
            att[
                s * rows_each : (s + 1) * rows_each, g * HEAD_SIZE : (g + 1) * HEAD_SIZE
            ] = blend_rows[:, s * group + g, :].astype(BF16)

    load_ow.wait()

    def project(p):
        columns = pl.ds(pl.multiple_of(p * width, 128), width)
        return jnp.dot(att[...], ow_v[:, columns], preferred_element_type=F32)

    sent_out = []
    for d in order:
        out_send[d] = project(peers[d]).astype(BF16)
        sent_out.append(to_z(5, d, out_send.at[d], out_recv.at[d]))
    result = project(t)
    for d in order:
        sent_out[d].wait_recv()
        result = result + out_recv[d].astype(F32)
    out_final[...] = result.astype(BF16)
    last = pltpu.make_async_copy(out_final, layer_out, store_sem.at[6])
    last.start()
    for copy in (
        g1 + g2 + gs + passed + sent_x + sent_factors + sent_keys + sent_values + sent_kv + sent_out
    ):
        copy.wait_send()
    for copy in stores:
        copy.wait()
    last.wait()


def fused_shards(
    layer_input_states,
    base_query_weight,
    key_value_weight,
    output_weight,
    stored_keys,
    stored_values,
    lengths,
    adapter_down,
    down_first_moment,
    down_second_moment,
    down_gradients,
    adapter_up,
    up_first_moment,
    up_second_moment,
    up_gradients,
):
    z = lax.axis_size("tensor")
    steps, rows, width = layer_input_states.shape
    rank = adapter_down.shape[0]
    columns = base_query_weight.shape[1]
    group = columns // HEAD_SIZE
    flat = steps * rows
    context = stored_keys.shape[2]
    place = jax.ShapeDtypeStruct
    down = adapter_down.shape
    up = adapter_up.shape
    down_half = (rank // 2, down[1])
    up_half = (rank // 2, up[1])
    seen = jnp.broadcast_to(lengths[:, None, None], (rows, steps * group, z * context))
    whole = pl.BlockSpec(memory_space=pl.ANY)
    in_specs = [whole] * 6 + [pl.BlockSpec(memory_space=pltpu.VMEM)] + [whole] * 8
    vm = pltpu.VMEM
    dma = pltpu.SemaphoreType.DMA
    results = pl.pallas_call(
        functools.partial(fused_kernel, z),
        out_shape=[place(down, F32)] * 3 + [place(up, F32)] * 3 + [place((flat, width), BF16)],
        in_specs=in_specs,
        out_specs=[whole] * 7,
        scratch_shapes=[
            vm((z, flat, width), BF16),
            vm((z, flat, width), BF16),
            vm(base_query_weight.shape, BF16),
            vm(key_value_weight.shape, BF16),
            vm(output_weight.shape, BF16),
            vm((z, rows, context, HEAD_SIZE), BF16),
            vm((z, rows, context, HEAD_SIZE), BF16),
            vm(down, F32),
            vm(down, F32),
            vm(down, F32),
            vm(up, F32),
            vm(up, F32),
            vm(up, F32),
            vm(down, F32),
            vm(up, F32),
            vm(down_half, F32),
            vm(up_half, F32),
            vm(down_half, F32),
            vm(up_half, F32),
            vm(down_half, F32),
            vm(up_half, F32),
            vm(down, F32),
            vm(up, F32),
            vm((z, 2, rank, width), BF16),
            vm((4 * rank, columns), BF16),
            vm((z, flat, 2 * HEAD_SIZE), F32),
            vm((z, flat, 2 * HEAD_SIZE), F32),
            vm((flat, columns), F32),
            vm((rows, steps * group, HEAD_SIZE), F32),
            vm((rows, steps * group, HEAD_SIZE), F32),
            vm((flat, columns), BF16),
            vm((z - 1, flat, width), BF16),
            vm((z - 1, flat, width), BF16),
            vm((flat, width), BF16),
            dma((14,)),
            dma((7,)),
            dma((6, z - 1)),
            dma((6, z - 1)),
            dma((6 + z - 1,)),
            dma((6 + z - 1,)),
        ],
        compiler_params=pltpu.CompilerParams(
            collective_id=0, has_side_effects=True, vmem_limit_bytes=56 * 1024 * 1024
        ),
    )(
        layer_input_states.reshape(flat, width),
        base_query_weight,
        key_value_weight,
        output_weight,
        stored_keys,
        stored_values,
        seen,
        adapter_down,
        down_first_moment,
        down_second_moment,
        down_gradients[0],
        adapter_up,
        up_first_moment,
        up_second_moment,
        up_gradients[0],
    )
    return (*results[:6], results[6].reshape(steps, rows, width))


def solution(mesh):
    local_heads = KEY_VALUE_HEADS == mesh.shape["tensor"] and mesh.shape["dp"] == 4
    shards = fused_shards if local_heads else general_shards
    in_specs = (
        P(None, ("parts", "dp"), "tensor"),
        P(None, "tensor"),
        P("tensor", None),
        P("tensor", None),
        P(None, ("parts", "dp"), "tensor", None),
        P(None, ("parts", "dp"), "tensor", None),
        P(("parts", "dp")),
        P(None, ("parts", "tensor")),
        P(None, ("parts", "tensor")),
        P(None, ("parts", "tensor")),
        P("dp", None, ("parts", "tensor")),
        P(None, ("parts", "tensor")),
        P(None, ("parts", "tensor")),
        P(None, ("parts", "tensor")),
        P("dp", None, ("parts", "tensor")),
    )
    out_specs = (
        P(None, ("parts", "tensor")),
        P(None, ("parts", "tensor")),
        P(None, ("parts", "tensor")),
        P(None, ("parts", "tensor")),
        P(None, ("parts", "tensor")),
        P(None, ("parts", "tensor")),
        P(None, ("parts", "dp"), "tensor"),
    )
    return jax.shard_map(shards, mesh=mesh, in_specs=in_specs, out_specs=out_specs, check_vma=False)
```

```python
import functools

import jax
import jax.numpy as jnp
from jax import lax
from jax.experimental import pallas as pl
from jax.experimental.pallas import tpu as pltpu
from jax.sharding import PartitionSpec as P

QUERY_HEAD_COUNT = 32
KEY_VALUE_HEADS = 4
HEAD_SIZE = 128


beta_one = 0.9
beta_two = 0.999
learn_rate = 0.01
adam_eps = 1e-08
bias_one = 1.0 - (0.9**50) ** 2
bias_two = 1.0 - (0.999**50) ** 2
adapter_scale = 2.0
norm_eps = 1e-06


def moment_optimizer_update(param, moment, second_moment, grad):
    moment_new = beta_one * moment + (1.0 - beta_one) * grad
    second_new = beta_two * second_moment + (1.0 - beta_two) * grad * grad
    step_size = moment_new / bias_one / (jnp.sqrt(second_new / bias_two) + adam_eps)
    return (param - learn_rate * step_size, moment_new, second_new)


def general_shards(
    layer_input_states,
    base_query_weight,
    key_value_weight,
    output_weight,
    stored_keys,
    stored_values,
    lengths,
    adapter_down,
    down_first_moment,
    down_second_moment,
    down_gradients,
    adapter_up,
    up_first_moment,
    up_second_moment,
    up_gradients,
):
    tensor_count = lax.axis_size("tensor")
    tensor_rank = lax.axis_index("tensor")
    summed_down_gradient, summed_up_gradient = lax.psum((down_gradients[0], up_gradients[0]), "dp")
    adapter_down_next, down_first_moment_next, down_second_moment_next = moment_optimizer_update(
        adapter_down, down_first_moment, down_second_moment, summed_down_gradient
    )
    adapter_up_next, up_first_moment_next, up_second_moment_next = moment_optimizer_update(
        adapter_up, up_first_moment, up_second_moment, summed_up_gradient
    )
    plain_query_rows = base_query_weight.astype(jnp.float32)
    factor_update = lax.dot_general(
        lax.all_gather(adapter_down_next, "tensor", axis=1, tiled=True),
        adapter_up_next,
        (((0,), (0,)), ((), ())),
        precision=lax.Precision.HIGHEST,
        preferred_element_type=jnp.float32,
    )
    merged_query_weight = (plain_query_rows + adapter_scale * factor_update).astype(jnp.bfloat16)
    heads_local = QUERY_HEAD_COUNT // tensor_count
    local_ctx = stored_keys.shape[2]
    slot_index = tensor_rank * local_ctx + jnp.arange(local_ctx, dtype=jnp.int32)
    score_scale = HEAD_SIZE ** (-0.5)
    key_cache = stored_keys
    value_cache = stored_values
    pieces = []
    for step_index in range(layer_input_states.shape[0]):
        hidden_block = layer_input_states[step_index : step_index + 1]
        decode_key_cache = key_cache
        decode_value_cache = value_cache
        optimizer_step_count = hidden_block.shape[0]
        decode_row_count = hidden_block.shape[1]
        gathered = lax.all_gather(hidden_block, "tensor", axis=2, tiled=True)
        widened = gathered.astype(jnp.float32)
        inverse = lax.rsqrt(jnp.mean(widened * widened, axis=-1, keepdims=True) + norm_eps)
        normed = (widened * inverse).astype(jnp.bfloat16)
        normed_local = (hidden_block.astype(jnp.float32) * inverse).astype(jnp.bfloat16)
        partial_kv = jnp.einsum(
            "srd,de->sre", normed_local, key_value_weight, preferred_element_type=jnp.float32
        )
        key_value_rows = lax.psum(partial_kv, "tensor").astype(jnp.bfloat16)
        key_value_rows = key_value_rows.reshape(
            optimizer_step_count, decode_row_count, 2, KEY_VALUE_HEADS, HEAD_SIZE
        )
        queries_local = jnp.einsum(
            "srd,de->sre", normed, merged_query_weight, preferred_element_type=jnp.float32
        ).astype(jnp.bfloat16)
        query_rows = lax.all_gather(queries_local, "tensor", axis=2, tiled=True)
        query_rows = query_rows.reshape(
            optimizer_step_count,
            decode_row_count,
            KEY_VALUE_HEADS,
            QUERY_HEAD_COUNT // KEY_VALUE_HEADS,
            HEAD_SIZE,
        )
        written = (slot_index[None, :] == lengths[:, None] + step_index + 0)[None, :, :, None]
        new_keys = jnp.transpose(key_value_rows[0, :, 0], (1, 0, 2))[:, :, None, :]
        new_values = jnp.transpose(key_value_rows[0, :, 1], (1, 0, 2))[:, :, None, :]
        decode_key_cache = jnp.where(written, new_keys, decode_key_cache)
        decode_value_cache = jnp.where(written, new_values, decode_value_cache)
        step_offsets = step_index + 1 + jnp.arange(optimizer_step_count, dtype=jnp.int32)
        visible = slot_index[None, None, :] < lengths[None, :, None] + step_offsets[:, None, None]
        visible = visible[:, None, None, :, :]
        scores = (
            jnp.einsum(
                "srhgd,hrcd->shgrc",
                query_rows,
                decode_key_cache,
                preferred_element_type=jnp.float32,
            )
            * score_scale
        )
        scores = jnp.where(visible, scores, -1e30)
        row_max = jnp.max(scores, axis=-1)
        weights = jnp.where(visible, jnp.exp(scores - row_max[..., None]), 0.0)
        totals = jnp.sum(weights, axis=-1)
        blended = jnp.einsum(
            "shgrc,hrcd->shgrd",
            weights.astype(jnp.bfloat16),
            decode_value_cache,
            preferred_element_type=jnp.float32,
        )
        blended = blended.reshape(
            optimizer_step_count, tensor_count, heads_local, decode_row_count, HEAD_SIZE
        )
        row_max = row_max.reshape(optimizer_step_count, tensor_count, heads_local, decode_row_count)
        totals = totals.reshape(optimizer_step_count, tensor_count, heads_local, decode_row_count)
        blended_in = lax.all_to_all(blended, "tensor", split_axis=1, concat_axis=1, tiled=True)
        peak_scores = lax.all_to_all(row_max, "tensor", split_axis=1, concat_axis=1, tiled=True)
        masses = lax.all_to_all(totals, "tensor", split_axis=1, concat_axis=1, tiled=True)
        overall = jnp.max(peak_scores, axis=1, keepdims=True)
        factor = jnp.exp(peak_scores - overall)
        denominator = jnp.sum(factor * masses, axis=1)
        combined = jnp.sum(factor[..., None] * blended_in, axis=1) / denominator[..., None]
        combined = jnp.transpose(combined, (0, 2, 1, 3))
        attended = combined.reshape(
            combined.shape[0], combined.shape[1], heads_local * HEAD_SIZE
        ).astype(jnp.bfloat16)
        projected = jnp.einsum(
            "sre,ed->srd", attended, output_weight, preferred_element_type=jnp.float32
        )
        reduced = lax.psum_scatter(projected, "tensor", scatter_dimension=2, tiled=True)
        step_out = reduced.astype(jnp.bfloat16)
        key_cache = decode_key_cache
        value_cache = decode_value_cache
        pieces.append(step_out)
    layer_out = jnp.concatenate(pieces, axis=0)
    return (
        adapter_down_next,
        down_first_moment_next,
        down_second_moment_next,
        adapter_up_next,
        up_first_moment_next,
        up_second_moment_next,
        layer_out,
    )


MESH = pl.DeviceIdType.MESH
F32 = jnp.float32
BF16 = jnp.bfloat16


def split_high_low(value):
    high = value.astype(BF16)
    return high, (value - high.astype(F32)).astype(BF16)


def fused_kernel(
    shards_z,
    x_in,
    base_in,
    kvw_in,
    ow_in,
    keys_in,
    values_in,
    lengths_ref,
    pd_in,
    md_in,
    vd_in,
    gd_in,
    pu_in,
    mu_in,
    vu_in,
    gu_in,
    pd_out,
    md_out,
    vd_out,
    pu_out,
    mu_out,
    vu_out,
    layer_out,
    xg,
    normed,
    base_v,
    kvw_v,
    ow_v,
    keys_v,
    values_v,
    pd,
    md,
    vd,
    pu,
    mu,
    vu,
    gd,
    gu,
    g1d,
    g1u,
    g2d,
    g2u,
    r2d,
    r2u,
    gsd,
    gsu,
    factors,
    up_cat,
    kv_send,
    kv_recv,
    q_acc,
    q_rows,
    blend_rows,
    att,
    out_send,
    out_recv,
    out_wide,
    out_final,
    load_sem,
    store_sem,
    z_send,
    z_recv,
    pair_send,
    pair_recv,
    hop_send,
    hop_recv,
):
    t = lax.axis_index("tensor")
    replica = lax.axis_index("dp")
    half = lax.rem(replica, 2)
    other = 1 - half
    mate = replica + 1 - 2 * half
    across = lax.rem(replica + 2, 4)
    rank = pd.shape[0]
    hr = rank // 2
    qr = rank // 4
    side = replica // 2
    quarter = half * 2 + side
    beside = half * 2 + 1 - side
    width = xg.shape[2]
    steps_rows = xg.shape[1]

    def quarter_rows(q):
        return pl.ds(pl.multiple_of(q * qr, qr), qr)

    mine = pl.ds(pl.multiple_of(half * hr, hr), hr)
    theirs = pl.ds(pl.multiple_of(other * hr, hr), hr)
    peers = [lax.rem(t + d, shards_z) for d in range(1, shards_z)]
    sources = [lax.rem(t + shards_z - d, shards_z) for d in range(1, shards_z)]
    order = range(shards_z - 1)

    def load(index, src, dst):
        copy = pltpu.make_async_copy(src, dst, load_sem.at[index])
        copy.start()
        return copy

    def to_z(kind, d, src, dst):
        copy = pltpu.make_async_remote_copy(
            src_ref=src,
            dst_ref=dst,
            send_sem=z_send.at[kind, d],
            recv_sem=z_recv.at[kind, d],
            device_id={"tensor": peers[d]},
            device_id_type=MESH,
        )
        copy.start()
        return copy

    def to_dp(index, target, src, dst):
        copy = pltpu.make_async_remote_copy(
            src_ref=src,
            dst_ref=dst,
            send_sem=pair_send.at[index],
            recv_sem=pair_recv.at[index],
            device_id={"dp": target},
            device_id_type=MESH,
        )
        copy.start()
        return copy

    def hop_copy(way, k, block, first):
        return pltpu.make_async_remote_copy(
            src_ref=x_in if first else xg.at[block],
            dst_ref=xg.at[block],
            send_sem=hop_send.at[way, k - 1],
            recv_sem=hop_recv.at[way, k - 1],
            device_id={"tensor": peers[0] if way == 0 else sources[0]},
            device_id_type=MESH,
        )

    def hop_sends(way, k):
        if way == 0:
            return (t < shards_z - 1) & (t >= k - 1), sources[k - 2] if k > 1 else t
        return (t > 0) & (t + k <= shards_z), peers[k - 2] if k > 1 else t

    def hop_start(k):
        for way in range(2):
            sends, block = hop_sends(way, k)

            @pl.when(sends)
            def _(way=way, block=block):
                hop_copy(way, k, block, k == 1).start()

    def hop_finish(k):
        for way in range(2):
            sends, block = hop_sends(way, k)

            @pl.when(sends)
            def _(way=way, block=block):
                hop_copy(way, k, block, k == 1).wait_send()

    def hop_arrive(k):
        for way in range(2):
            gets = t >= k if way == 0 else t + k < shards_z

            @pl.when(gets)
            def _(way=way):
                block = sources[k - 1] if way == 0 else peers[k - 1]
                hop_copy(way, k, block, False).wait_recv()

    barrier = pltpu.get_barrier_semaphore()
    for p in peers:
        pl.semaphore_signal(barrier, inc=1, device_id={"tensor": p}, device_id_type=MESH)
    for p in (mate, across):
        pl.semaphore_signal(barrier, inc=1, device_id={"dp": p}, device_id_type=MESH)
    load_gd = load(0, gd_in, gd)
    load_gu = load(1, gu_in, gu)
    adam_loads = [
        load(2 + i, a, b)
        for i, (a, b) in enumerate(
            ((pd_in, pd), (md_in, md), (vd_in, vd), (pu_in, pu), (mu_in, mu), (vu_in, vu))
        )
    ]
    load_x = load(8, x_in, xg.at[t])
    load_kvw = load(9, kvw_in, kvw_v)
    load_base = load(10, base_in, base_v)
    load_keys = load(11, keys_in.at[t], keys_v.at[t])
    load_values = load(12, values_in.at[t], values_v.at[t])
    load_ow = load(13, ow_in, ow_v)
    pl.semaphore_wait(barrier, shards_z + 1)

    g1 = [
        to_dp(0, mate, gd_in.at[theirs], g1d),
        to_dp(1, mate, gu_in.at[theirs], g1u),
    ]
    hop_start(1)

    load_gd.wait()
    load_gu.wait()
    for copy in g1:
        copy.wait_recv()
    g2d[...] = gd[mine, :] + g1d[...]
    g2u[...] = gu[mine, :] + g1u[...]
    kept = quarter_rows(side)
    given = quarter_rows(1 - side)
    g2 = [to_dp(2, across, g2d.at[given], r2d), to_dp(3, across, g2u.at[given], r2u)]
    hop_arrive(1)
    hop_start(2)
    for copy in adam_loads:
        copy.wait()
    for copy in g2:
        copy.wait_recv()
    own = quarter_rows(quarter)
    next_to = quarter_rows(beside)
    gsd[own, :] = g2d[kept, :] + r2d[...]
    gsu[own, :] = g2u[kept, :] + r2u[...]
    gs = [
        to_dp(4, across, gsd.at[own], gsd.at[own]),
        to_dp(5, across, gsu.at[own], gsu.at[own]),
    ]
    gm = [
        to_dp(6, mate, gsd.at[own], gsd.at[own]),
        to_dp(7, mate, gsu.at[own], gsu.at[own]),
    ]

    def step_down(q):
        rows = quarter_rows(q)
        new = moment_optimizer_update(pd[rows, :], md[rows, :], vd[rows, :], gsd[rows, :])
        pd[rows, :], md[rows, :], vd[rows, :] = new
        high, low = split_high_low(new[0])
        factors[t, q, 0:qr, :] = high
        factors[t, q, qr : 2 * qr, :] = low

    step_down(quarter)
    sent_factors = [to_z(0, d, factors.at[t, quarter], factors.at[t, quarter]) for d in order]
    hop_arrive(2)
    hop_start(3)
    parts_of_rows = 2
    rows_each = q_rows.shape[0]
    rows_part = rows_each // parts_of_rows

    def send_caches(part):
        cut = pl.ds(part * rows_part, rows_part)
        return [
            to_z(2 + 2 * part + i, d, source.at[peers[d], cut], held.at[t, cut])
            for d in order
            for i, (source, held) in enumerate(((keys_in, keys_v), (values_in, values_v)))
        ]

    sent_caches = [send_caches(0)]
    for copy in gs:
        copy.wait_recv()
    gm += [
        to_dp(8, mate, gsd.at[next_to], gsd.at[next_to]),
        to_dp(9, mate, gsu.at[next_to], gsu.at[next_to]),
    ]
    step_down(beside)
    for copy in gm:
        copy.wait_recv()
    step_down(other * 2)
    step_down(other * 2 + 1)
    new_up = moment_optimizer_update(pu[...], mu[...], vu[...], gsu[...])
    pu[...], mu[...], vu[...] = new_up
    stores = []
    for i, (a, b) in enumerate(
        ((pd, pd_out), (md, md_out), (vd, vd_out), (pu, pu_out), (mu, mu_out), (vu, vu_out))
    ):
        copy = pltpu.make_async_copy(a, b, store_sem.at[i])
        copy.start()
        stores.append(copy)
    up_parts = split_high_low(adapter_scale * new_up[0])
    for i in range(2):
        for j in range(4):
            piece = up_parts[i][j * qr : (j + 1) * qr, :]
            at = (i * 4 + j) * 2 * qr
            up_cat[at : at + qr, :] = piece
            up_cat[at + qr : at + 2 * qr, :] = piece

    load_x.wait()
    hop_arrive(3)
    squares = jnp.zeros((steps_rows, 1), F32)
    for b in range(shards_z):
        wide = xg[b].astype(F32)
        squares = squares + jnp.sum(wide * wide, axis=-1, keepdims=True)
    inverse = lax.rsqrt(squares / (width * shards_z) + norm_eps)
    for b in range(shards_z):
        normed[b] = (xg[b].astype(F32) * inverse).astype(BF16)
    load_kvw.wait()
    local_rows = normed[t]
    kv_half = KEY_VALUE_HEADS * HEAD_SIZE
    for p in range(shards_z):
        for kind in range(2):
            at = kind * kv_half + p * HEAD_SIZE
            kv_send[p, :, kind * HEAD_SIZE : (kind + 1) * HEAD_SIZE] = jnp.dot(
                local_rows, kvw_v[:, at : at + HEAD_SIZE], preferred_element_type=F32
            )
    sent_kv = [to_z(1, d, kv_send.at[peers[d]], kv_recv.at[t]) for d in order]
    sent_caches.append(send_caches(1))

    load_base.wait()
    q_acc[...] = jnp.zeros_like(q_acc)
    tile = 256

    def query_block(b):
        def body(j, carry):
            columns = pl.ds(pl.multiple_of(j * tile, tile), tile)
            left = factors[b, :, :, columns].reshape(2 * rank, tile)
            update = lax.dot_general(
                jnp.concatenate([left, left], axis=0),
                up_cat[...],
                (((0,), (0,)), ((), ())),
                preferred_element_type=F32,
            )
            rows = pl.ds(pl.multiple_of(b * width + j * tile, tile), tile)
            merged = (base_v[rows, :].astype(F32) + update).astype(BF16)
            q_acc[...] += jnp.dot(normed[b, :, columns], merged, preferred_element_type=F32)
            return carry

        lax.fori_loop(0, width // tile, body, 0)

    query_block(t)
    passed = []
    crossed = []
    for d in order:
        sent_factors[d].wait_recv()
        slot = factors.at[sources[d], quarter]
        crossed.append(to_dp(10 + 3 * d, across, slot, slot))
        passed.append(to_dp(11 + 3 * d, mate, slot, slot))
    for d in order:
        crossed[d].wait_recv()
        slot = factors.at[sources[d], beside]
        passed.append(to_dp(12 + 3 * d, mate, slot, slot))
    for d in order:
        passed[d].wait_recv()
        passed[shards_z - 1 + d].wait_recv()
        query_block(sources[d])

    steps = steps_rows // rows_each
    group = q_acc.shape[1] // HEAD_SIZE
    rounded = q_acc[...].astype(BF16).astype(F32)
    for s in range(steps):
        for g in range(group):
            q_rows[:, s * group + g, :] = rounded[
                s * rows_each : (s + 1) * rows_each, g * HEAD_SIZE : (g + 1) * HEAD_SIZE
            ]
    for copy in sent_kv:
        copy.wait_recv()
    new_kv = kv_send[t]
    for d in order:
        new_kv = new_kv + kv_recv[sources[d]]
    new_kv = new_kv.astype(BF16)
    new_keys = new_kv[:, :HEAD_SIZE]
    new_values = new_kv[:, HEAD_SIZE:]
    load_keys.wait()
    load_values.wait()
    load_ow.wait()
    scale = HEAD_SIZE ** (-0.5)
    pairs = steps * group
    flat_part = rows_part * pairs
    steps_part = steps * rows_part
    sent_out = []
    results = []

    def project(p):
        columns = pl.ds(pl.multiple_of(p * width, 128), width)
        return jnp.dot(att[...].astype(BF16), ow_v[:, columns], preferred_element_type=F32)

    for part in range(parts_of_rows):
        for copy in sent_caches[part]:
            copy.wait_recv()
        cut = slice(part * rows_part, (part + 1) * rows_part)
        queries = q_rows[cut].astype(BF16)
        keys = jnp.concatenate([keys_v[b, cut] for b in range(shards_z)], axis=1)
        values = jnp.concatenate([values_v[b, cut] for b in range(shards_z)], axis=1)
        old = (
            lax.dot_general(
                queries, keys, (((2,), (2,)), ((0,), (0,))), preferred_element_type=F32
            )
            * scale
        )
        fresh = (
            lax.dot_general(
                queries.reshape(flat_part, HEAD_SIZE),
                new_keys,
                (((1,), (1,)), ((), ())),
                preferred_element_type=F32,
            )
            * scale
        ).reshape(rows_part, pairs, steps_rows)
        place = lax.broadcasted_iota(jnp.int32, old.shape, 2)
        filled = [
            jnp.full((1, 1, old.shape[2]), lengths_ref[part * rows_part + r], jnp.int32)
            for r in range(rows_part)
        ]
        seen_old = place < jnp.concatenate(filled, axis=0)
        column = lax.broadcasted_iota(jnp.int32, fresh.shape, 2)
        row = lax.broadcasted_iota(jnp.int32, fresh.shape, 0) + part * rows_part
        step = lax.broadcasted_iota(jnp.int32, fresh.shape, 1) // group
        seen_new = (column % rows_each == row) & (column // rows_each <= step)
        old = jnp.where(seen_old, old, -1e30)
        fresh = jnp.where(seen_new, fresh, -1e30)
        peak = jnp.maximum(
            jnp.max(old, axis=-1, keepdims=True), jnp.max(fresh, axis=-1, keepdims=True)
        )
        old = jnp.where(seen_old, jnp.exp(old - peak), 0.0)
        fresh = jnp.where(seen_new, jnp.exp(fresh - peak), 0.0)
        total = jnp.sum(old, axis=-1, keepdims=True) + jnp.sum(fresh, axis=-1, keepdims=True)
        blended = lax.dot_general(
            old.astype(BF16), values, (((2,), (1,)), ((0,), (0,))), preferred_element_type=F32
        )
        blended = blended + jnp.dot(
            fresh.reshape(flat_part, steps_rows).astype(BF16),
            new_values,
            preferred_element_type=F32,
        ).reshape(rows_part, pairs, HEAD_SIZE)
        blend_rows[...] = blended / total
        for s in range(steps):
            for g in range(group):
                att[
                    s * rows_part : (s + 1) * rows_part, g * HEAD_SIZE : (g + 1) * HEAD_SIZE
                ] = blend_rows[:, s * group + g, :]
        for d in order:
            out_send[part, d] = project(peers[d]).astype(BF16)
            sent_out.append(
                to_z(6 + part, d, out_send.at[part, d], out_recv.at[part, d])
            )
        results.append(project(t))
    for part in range(parts_of_rows):
        result = results[part]
        for d in order:
            sent_out[part * (shards_z - 1) + d].wait_recv()
            result = result + out_recv[part, d].astype(F32)
        for s in range(steps):
            at = s * rows_each + part * rows_part
            out_wide[at : at + rows_part, :] = result[s * rows_part : (s + 1) * rows_part, :]
    out_final[...] = out_wide[...].astype(BF16)
    last = pltpu.make_async_copy(out_final, layer_out, store_sem.at[6])
    last.start()
    for k in range(1, shards_z):
        hop_finish(k)
    for copy in g1 + g2 + gs + gm + passed + crossed + sent_factors + sent_kv + sent_out:
        copy.wait_send()
    for copies in sent_caches:
        for copy in copies:
            copy.wait_send()
    for copy in stores:
        copy.wait()
    last.wait()


def write_kernel(count, *refs):
    sources, targets, held = (refs[i * count : (i + 1) * count] for i in range(3))
    sem = refs[-1]
    reads = [pltpu.make_async_copy(sources[i], held[i], sem.at[0, i]) for i in range(count)]
    writes = [pltpu.make_async_copy(held[i], targets[i], sem.at[1, i]) for i in range(count)]
    for copy in reads:
        copy.start()
    for read, write in zip(reads, writes):
        read.wait()
        write.start()
    for copy in writes:
        copy.wait()


def fused_shards(
    layer_input_states,
    base_query_weight,
    key_value_weight,
    output_weight,
    stored_keys,
    stored_values,
    lengths,
    adapter_down,
    down_first_moment,
    down_second_moment,
    down_gradients,
    adapter_up,
    up_first_moment,
    up_second_moment,
    up_gradients,
):
    z = lax.axis_size("tensor")
    steps, rows, width = layer_input_states.shape
    rank = adapter_down.shape[0]
    columns = base_query_weight.shape[1]
    group = columns // HEAD_SIZE
    flat = steps * rows
    context = stored_keys.shape[2]
    place = jax.ShapeDtypeStruct
    down = adapter_down.shape
    up = adapter_up.shape
    down_half = (rank // 2, down[1])
    up_half = (rank // 2, up[1])
    whole = pl.BlockSpec(memory_space=pl.ANY)
    in_specs = [whole] * 6 + [pl.BlockSpec(memory_space=pltpu.SMEM)] + [whole] * 8
    vm = pltpu.VMEM
    dma = pltpu.SemaphoreType.DMA
    results = pl.pallas_call(
        functools.partial(fused_kernel, z),
        out_shape=[place(down, F32)] * 3 + [place(up, F32)] * 3 + [place((flat, width), BF16)],
        in_specs=in_specs,
        out_specs=[whole] * 7,
        scratch_shapes=[
            vm((z, flat, width), BF16),
            vm((z, flat, width), BF16),
            vm(base_query_weight.shape, BF16),
            vm(key_value_weight.shape, BF16),
            vm(output_weight.shape, BF16),
            vm((z, rows, context, HEAD_SIZE), BF16),
            vm((z, rows, context, HEAD_SIZE), BF16),
            vm(down, F32),
            vm(down, F32),
            vm(down, F32),
            vm(up, F32),
            vm(up, F32),
            vm(up, F32),
            vm(down, F32),
            vm(up, F32),
            vm(down_half, F32),
            vm(up_half, F32),
            vm(down_half, F32),
            vm(up_half, F32),
            vm((rank // 4, down[1]), F32),
            vm((rank // 4, up[1]), F32),
            vm(down, F32),
            vm(up, F32),
            vm((z, 4, rank // 2, width), BF16),
            vm((4 * rank, columns), BF16),
            vm((z, flat, 2 * HEAD_SIZE), F32),
            vm((z, flat, 2 * HEAD_SIZE), F32),
            vm((flat, columns), F32),
            vm((rows, steps * group, HEAD_SIZE), F32),
            vm((rows // 2, steps * group, HEAD_SIZE), F32),
            vm((flat // 2, columns), F32),
            vm((2, z - 1, flat // 2, width), BF16),
            vm((2, z - 1, flat // 2, width), BF16),
            vm((flat, width), F32),
            vm((flat, width), BF16),
            dma((14,)),
            dma((7,)),
            dma((8, z - 1)),
            dma((8, z - 1)),
            dma((10 + 3 * (z - 1),)),
            dma((10 + 3 * (z - 1),)),
            dma((2, z - 1)),
            dma((2, z - 1)),
        ],
        compiler_params=pltpu.CompilerParams(
            collective_id=0, has_side_effects=True, vmem_limit_bytes=56 * 1024 * 1024
        ),
    )(
        layer_input_states.reshape(flat, width),
        base_query_weight,
        key_value_weight,
        output_weight,
        stored_keys,
        stored_values,
        lengths,
        adapter_down,
        down_first_moment,
        down_second_moment,
        down_gradients[0],
        adapter_up,
        up_first_moment,
        up_second_moment,
        up_gradients[0],
    )
    results = pl.pallas_call(
        functools.partial(write_kernel, 7),
        out_shape=[place(r.shape, r.dtype) for r in results],
        in_specs=[whole] * 7,
        out_specs=[whole] * 7,
        scratch_shapes=[vm(r.shape, r.dtype) for r in results] + [dma((2, 7))],
        compiler_params=pltpu.CompilerParams(vmem_limit_bytes=32 * 1024 * 1024),
    )(*results)
    return (*results[:6], results[6].reshape(steps, rows, width))


def solution(mesh):
    local_heads = KEY_VALUE_HEADS == mesh.shape["tensor"] and mesh.shape["dp"] == 4
    shards = fused_shards if local_heads else general_shards
    in_specs = (
        P(None, ("parts", "dp"), "tensor"),
        P(None, "tensor"),
        P("tensor", None),
        P("tensor", None),
        P(None, ("parts", "dp"), "tensor", None),
        P(None, ("parts", "dp"), "tensor", None),
        P(("parts", "dp")),
        P(None, ("parts", "tensor")),
        P(None, ("parts", "tensor")),
        P(None, ("parts", "tensor")),
        P("dp", None, ("parts", "tensor")),
        P(None, ("parts", "tensor")),
        P(None, ("parts", "tensor")),
        P(None, ("parts", "tensor")),
        P("dp", None, ("parts", "tensor")),
    )
    out_specs = (
        P(None, ("parts", "tensor")),
        P(None, ("parts", "tensor")),
        P(None, ("parts", "tensor")),
        P(None, ("parts", "tensor")),
        P(None, ("parts", "tensor")),
        P(None, ("parts", "tensor")),
        P(None, ("parts", "dp"), "tensor"),
    )
    return jax.shard_map(shards, mesh=mesh, in_specs=in_specs, out_specs=out_specs, check_vma=False)
```

```python
import functools

import jax
import jax.numpy as jnp
from jax import lax
from jax.experimental import pallas as pl
from jax.experimental.pallas import tpu as pltpu
from jax.sharding import PartitionSpec as P

QUERY_HEAD_COUNT = 32
KEY_VALUE_HEADS = 4
HEAD_SIZE = 128


beta_one = 0.9
beta_two = 0.999
learn_rate = 0.01
adam_eps = 1e-08
bias_one = 1.0 - (0.9**50) ** 2
bias_two = 1.0 - (0.999**50) ** 2
adapter_scale = 2.0
norm_eps = 1e-06


def moment_optimizer_update(param, moment, second_moment, grad):
    moment_new = beta_one * moment + (1.0 - beta_one) * grad
    second_new = beta_two * second_moment + (1.0 - beta_two) * grad * grad
    step_size = moment_new / bias_one / (jnp.sqrt(second_new / bias_two) + adam_eps)
    return (param - learn_rate * step_size, moment_new, second_new)


def general_shards(
    layer_input_states,
    base_query_weight,
    key_value_weight,
    output_weight,
    stored_keys,
    stored_values,
    lengths,
    adapter_down,
    down_first_moment,
    down_second_moment,
    down_gradients,
    adapter_up,
    up_first_moment,
    up_second_moment,
    up_gradients,
):
    tensor_count = lax.axis_size("tensor")
    tensor_rank = lax.axis_index("tensor")
    summed_down_gradient, summed_up_gradient = lax.psum((down_gradients[0], up_gradients[0]), "dp")
    adapter_down_next, down_first_moment_next, down_second_moment_next = moment_optimizer_update(
        adapter_down, down_first_moment, down_second_moment, summed_down_gradient
    )
    adapter_up_next, up_first_moment_next, up_second_moment_next = moment_optimizer_update(
        adapter_up, up_first_moment, up_second_moment, summed_up_gradient
    )
    plain_query_rows = base_query_weight.astype(jnp.float32)
    factor_update = lax.dot_general(
        lax.all_gather(adapter_down_next, "tensor", axis=1, tiled=True),
        adapter_up_next,
        (((0,), (0,)), ((), ())),
        precision=lax.Precision.HIGHEST,
        preferred_element_type=jnp.float32,
    )
    merged_query_weight = (plain_query_rows + adapter_scale * factor_update).astype(jnp.bfloat16)
    heads_local = QUERY_HEAD_COUNT // tensor_count
    local_ctx = stored_keys.shape[2]
    slot_index = tensor_rank * local_ctx + jnp.arange(local_ctx, dtype=jnp.int32)
    score_scale = HEAD_SIZE ** (-0.5)
    key_cache = stored_keys
    value_cache = stored_values
    pieces = []
    for step_index in range(layer_input_states.shape[0]):
        hidden_block = layer_input_states[step_index : step_index + 1]
        decode_key_cache = key_cache
        decode_value_cache = value_cache
        optimizer_step_count = hidden_block.shape[0]
        decode_row_count = hidden_block.shape[1]
        gathered = lax.all_gather(hidden_block, "tensor", axis=2, tiled=True)
        widened = gathered.astype(jnp.float32)
        inverse = lax.rsqrt(jnp.mean(widened * widened, axis=-1, keepdims=True) + norm_eps)
        normed = (widened * inverse).astype(jnp.bfloat16)
        normed_local = (hidden_block.astype(jnp.float32) * inverse).astype(jnp.bfloat16)
        partial_kv = jnp.einsum(
            "srd,de->sre", normed_local, key_value_weight, preferred_element_type=jnp.float32
        )
        key_value_rows = lax.psum(partial_kv, "tensor").astype(jnp.bfloat16)
        key_value_rows = key_value_rows.reshape(
            optimizer_step_count, decode_row_count, 2, KEY_VALUE_HEADS, HEAD_SIZE
        )
        queries_local = jnp.einsum(
            "srd,de->sre", normed, merged_query_weight, preferred_element_type=jnp.float32
        ).astype(jnp.bfloat16)
        query_rows = lax.all_gather(queries_local, "tensor", axis=2, tiled=True)
        query_rows = query_rows.reshape(
            optimizer_step_count,
            decode_row_count,
            KEY_VALUE_HEADS,
            QUERY_HEAD_COUNT // KEY_VALUE_HEADS,
            HEAD_SIZE,
        )
        written = (slot_index[None, :] == lengths[:, None] + step_index + 0)[None, :, :, None]
        new_keys = jnp.transpose(key_value_rows[0, :, 0], (1, 0, 2))[:, :, None, :]
        new_values = jnp.transpose(key_value_rows[0, :, 1], (1, 0, 2))[:, :, None, :]
        decode_key_cache = jnp.where(written, new_keys, decode_key_cache)
        decode_value_cache = jnp.where(written, new_values, decode_value_cache)
        step_offsets = step_index + 1 + jnp.arange(optimizer_step_count, dtype=jnp.int32)
        visible = slot_index[None, None, :] < lengths[None, :, None] + step_offsets[:, None, None]
        visible = visible[:, None, None, :, :]
        scores = (
            jnp.einsum(
                "srhgd,hrcd->shgrc",
                query_rows,
                decode_key_cache,
                preferred_element_type=jnp.float32,
            )
            * score_scale
        )
        scores = jnp.where(visible, scores, -1e30)
        row_max = jnp.max(scores, axis=-1)
        weights = jnp.where(visible, jnp.exp(scores - row_max[..., None]), 0.0)
        totals = jnp.sum(weights, axis=-1)
        blended = jnp.einsum(
            "shgrc,hrcd->shgrd",
            weights.astype(jnp.bfloat16),
            decode_value_cache,
            preferred_element_type=jnp.float32,
        )
        blended = blended.reshape(
            optimizer_step_count, tensor_count, heads_local, decode_row_count, HEAD_SIZE
        )
        row_max = row_max.reshape(optimizer_step_count, tensor_count, heads_local, decode_row_count)
        totals = totals.reshape(optimizer_step_count, tensor_count, heads_local, decode_row_count)
        blended_in = lax.all_to_all(blended, "tensor", split_axis=1, concat_axis=1, tiled=True)
        peak_scores = lax.all_to_all(row_max, "tensor", split_axis=1, concat_axis=1, tiled=True)
        masses = lax.all_to_all(totals, "tensor", split_axis=1, concat_axis=1, tiled=True)
        overall = jnp.max(peak_scores, axis=1, keepdims=True)
        factor = jnp.exp(peak_scores - overall)
        denominator = jnp.sum(factor * masses, axis=1)
        combined = jnp.sum(factor[..., None] * blended_in, axis=1) / denominator[..., None]
        combined = jnp.transpose(combined, (0, 2, 1, 3))
        attended = combined.reshape(
            combined.shape[0], combined.shape[1], heads_local * HEAD_SIZE
        ).astype(jnp.bfloat16)
        projected = jnp.einsum(
            "sre,ed->srd", attended, output_weight, preferred_element_type=jnp.float32
        )
        reduced = lax.psum_scatter(projected, "tensor", scatter_dimension=2, tiled=True)
        step_out = reduced.astype(jnp.bfloat16)
        key_cache = decode_key_cache
        value_cache = decode_value_cache
        pieces.append(step_out)
    layer_out = jnp.concatenate(pieces, axis=0)
    return (
        adapter_down_next,
        down_first_moment_next,
        down_second_moment_next,
        adapter_up_next,
        up_first_moment_next,
        up_second_moment_next,
        layer_out,
    )


MESH = pl.DeviceIdType.MESH
F32 = jnp.float32
BF16 = jnp.bfloat16


def split_high_low(value):
    high = value.astype(BF16)
    return high, (value - high.astype(F32)).astype(BF16)


def fused_kernel(
    shards_z,
    x_in,
    base_in,
    kvw_in,
    ow_in,
    keys_in,
    values_in,
    lengths_ref,
    pd_in,
    md_in,
    vd_in,
    gd_in,
    pu_in,
    mu_in,
    vu_in,
    gu_in,
    pd_out,
    md_out,
    vd_out,
    pu_out,
    mu_out,
    vu_out,
    layer_out,
    xg,
    normed,
    base_v,
    kvw_v,
    ow_v,
    keys_v,
    values_v,
    pd,
    md,
    vd,
    pu,
    mu,
    vu,
    gd,
    gu,
    b1d,
    b1u,
    b2d,
    b2u,
    g1d,
    g1u,
    g2d,
    g2u,
    r2d,
    r2u,
    gsd,
    gsu,
    factors,
    up_cat,
    kv_send,
    kv_recv,
    q_acc,
    q_rows,
    blend_rows,
    att,
    out_send,
    out_recv,
    out_wide,
    out_final,
    load_sem,
    store_sem,
    z_send,
    z_recv,
    pair_send,
    pair_recv,
    hop_send,
    hop_recv,
):
    t = lax.axis_index("tensor")
    replica = lax.axis_index("dp")
    half = lax.rem(replica, 2)
    other = 1 - half
    mate = replica + 1 - 2 * half
    across = lax.rem(replica + 2, 4)
    rank = pd.shape[0]
    hr = rank // 2
    qr = rank // 4
    side = replica // 2
    quarter = half * 2 + side
    beside = half * 2 + 1 - side
    width = xg.shape[2]
    steps_rows = xg.shape[1]

    def quarter_rows(q):
        return pl.ds(pl.multiple_of(q * qr, qr), qr)

    mine = pl.ds(pl.multiple_of(half * hr, hr), hr)
    theirs = pl.ds(pl.multiple_of(other * hr, hr), hr)
    peers = [lax.rem(t + d, shards_z) for d in range(1, shards_z)]
    sources = [lax.rem(t + shards_z - d, shards_z) for d in range(1, shards_z)]
    order = range(shards_z - 1)

    def load(index, src, dst):
        copy = pltpu.make_async_copy(src, dst, load_sem.at[index])
        copy.start()
        return copy

    def to_z(kind, d, src, dst):
        copy = pltpu.make_async_remote_copy(
            src_ref=src,
            dst_ref=dst,
            send_sem=z_send.at[kind, d],
            recv_sem=z_recv.at[kind, d],
            device_id={"tensor": peers[d]},
            device_id_type=MESH,
        )
        copy.start()
        return copy

    def to_dp(index, target, src, dst):
        copy = pltpu.make_async_remote_copy(
            src_ref=src,
            dst_ref=dst,
            send_sem=pair_send.at[index],
            recv_sem=pair_recv.at[index],
            device_id={"dp": target},
            device_id_type=MESH,
        )
        copy.start()
        return copy

    def hop_copy(way, k, block, first):
        return pltpu.make_async_remote_copy(
            src_ref=x_in if first else xg.at[block],
            dst_ref=xg.at[block],
            send_sem=hop_send.at[way, k - 1],
            recv_sem=hop_recv.at[way, k - 1],
            device_id={"tensor": peers[0] if way == 0 else sources[0]},
            device_id_type=MESH,
        )

    def hop_sends(way, k):
        if way == 0:
            return (t < shards_z - 1) & (t >= k - 1), sources[k - 2] if k > 1 else t
        return (t > 0) & (t + k <= shards_z), peers[k - 2] if k > 1 else t

    def hop_start(k):
        for way in range(2):
            sends, block = hop_sends(way, k)

            @pl.when(sends)
            def _(way=way, block=block):
                hop_copy(way, k, block, k == 1).start()

    def hop_finish(k):
        for way in range(2):
            sends, block = hop_sends(way, k)

            @pl.when(sends)
            def _(way=way, block=block):
                hop_copy(way, k, block, k == 1).wait_send()

    def hop_arrive(k):
        for way in range(2):
            gets = t >= k if way == 0 else t + k < shards_z

            @pl.when(gets)
            def _(way=way):
                block = sources[k - 1] if way == 0 else peers[k - 1]
                hop_copy(way, k, block, False).wait_recv()

    barrier = pltpu.get_barrier_semaphore()
    for p in peers:
        pl.semaphore_signal(barrier, inc=1, device_id={"tensor": p}, device_id_type=MESH)
    for p in (mate, across):
        pl.semaphore_signal(barrier, inc=1, device_id={"dp": p}, device_id_type=MESH)
    load_gd = load(0, gd_in, gd)
    load_gu = load(1, gu_in, gu)
    adam_loads = [
        load(2 + i, a, b)
        for i, (a, b) in enumerate(
            ((pd_in, pd), (md_in, md), (vd_in, vd), (pu_in, pu), (mu_in, mu), (vu_in, vu))
        )
    ]
    load_x = load(8, x_in, xg.at[t])
    load_kvw = load(9, kvw_in, kvw_v)
    load_base = load(10, base_in, base_v)
    load_keys = load(11, keys_in.at[t], keys_v.at[t])
    load_values = load(12, values_in.at[t], values_v.at[t])
    load_ow = load(13, ow_in, ow_v)
    pl.semaphore_wait(barrier, shards_z + 1)

    hop_start(1)

    load_gd.wait()
    load_gu.wait()
    b1d[...] = gd[theirs, :].astype(BF16)
    b1u[...] = gu[theirs, :].astype(BF16)
    g1 = [to_dp(0, mate, b1d, g1d), to_dp(1, mate, b1u, g1u)]
    for copy in g1:
        copy.wait_recv()
    g2d[...] = gd[mine, :] + g1d[...].astype(F32)
    g2u[...] = gu[mine, :] + g1u[...].astype(F32)
    b2d[...] = g2d[...].astype(BF16)
    b2u[...] = g2u[...].astype(BF16)
    kept = quarter_rows(side)
    given = quarter_rows(1 - side)
    g2 = [to_dp(2, across, b2d.at[given], r2d), to_dp(3, across, b2u.at[given], r2u)]
    hop_arrive(1)
    hop_start(2)
    parts_of_rows = 2
    rows_each = q_rows.shape[0]
    rows_part = rows_each // parts_of_rows

    def send_caches(part):
        cut = pl.ds(part * rows_part, rows_part)
        return [
            to_z(2 + 2 * part + i, d, source.at[peers[d], cut], held.at[t, cut])
            for d in order
            for i, (source, held) in enumerate(((keys_in, keys_v), (values_in, values_v)))
        ]

    sent_caches = [send_caches(0)]
    for copy in adam_loads:
        copy.wait()
    for copy in g2:
        copy.wait_recv()
    own = quarter_rows(quarter)
    next_to = quarter_rows(beside)
    gsd[own, :] = (g2d[kept, :] + r2d[...].astype(F32)).astype(BF16)
    gsu[own, :] = (g2u[kept, :] + r2u[...].astype(F32)).astype(BF16)
    gs = [
        to_dp(4, across, gsd.at[own], gsd.at[own]),
        to_dp(5, across, gsu.at[own], gsu.at[own]),
    ]
    gm = [
        to_dp(6, mate, gsd.at[own], gsd.at[own]),
        to_dp(7, mate, gsu.at[own], gsu.at[own]),
    ]

    def step_down(q):
        rows = quarter_rows(q)
        new = moment_optimizer_update(pd[rows, :], md[rows, :], vd[rows, :], gsd[rows, :].astype(F32))
        pd[rows, :], md[rows, :], vd[rows, :] = new
        high, low = split_high_low(new[0])
        factors[t, q, 0:qr, :] = high
        factors[t, q, qr : 2 * qr, :] = low

    step_down(quarter)
    sent_factors = [to_z(0, d, factors.at[t, quarter], factors.at[t, quarter]) for d in order]
    hop_arrive(2)
    hop_start(3)
    for copy in gs:
        copy.wait_recv()
    gm += [
        to_dp(8, mate, gsd.at[next_to], gsd.at[next_to]),
        to_dp(9, mate, gsu.at[next_to], gsu.at[next_to]),
    ]
    step_down(beside)
    for copy in gm:
        copy.wait_recv()
    step_down(other * 2)
    step_down(other * 2 + 1)
    new_up = moment_optimizer_update(pu[...], mu[...], vu[...], gsu[...].astype(F32))
    pu[...], mu[...], vu[...] = new_up
    stores = []
    for i, (a, b) in enumerate(
        ((pd, pd_out), (md, md_out), (vd, vd_out), (pu, pu_out), (mu, mu_out), (vu, vu_out))
    ):
        copy = pltpu.make_async_copy(a, b, store_sem.at[i])
        copy.start()
        stores.append(copy)
    up_parts = split_high_low(adapter_scale * new_up[0])
    for i in range(2):
        for j in range(4):
            piece = up_parts[i][j * qr : (j + 1) * qr, :]
            at = (i * 4 + j) * 2 * qr
            up_cat[at : at + qr, :] = piece
            up_cat[at + qr : at + 2 * qr, :] = piece

    load_x.wait()
    hop_arrive(3)
    squares = jnp.zeros((steps_rows, 1), F32)
    for b in range(shards_z):
        wide = xg[b].astype(F32)
        squares = squares + jnp.sum(wide * wide, axis=-1, keepdims=True)
    inverse = lax.rsqrt(squares / (width * shards_z) + norm_eps)
    for b in range(shards_z):
        normed[b] = (xg[b].astype(F32) * inverse).astype(BF16)
    load_kvw.wait()
    local_rows = normed[t]
    kv_half = KEY_VALUE_HEADS * HEAD_SIZE
    for p in range(shards_z):
        for kind in range(2):
            at = kind * kv_half + p * HEAD_SIZE
            kv_send[p, :, kind * HEAD_SIZE : (kind + 1) * HEAD_SIZE] = jnp.dot(
                local_rows, kvw_v[:, at : at + HEAD_SIZE], preferred_element_type=F32
            )
    sent_kv = [to_z(1, d, kv_send.at[peers[d]], kv_recv.at[t]) for d in order]
    sent_caches.append(send_caches(1))

    load_base.wait()
    q_acc[...] = jnp.zeros_like(q_acc)
    tile = 256

    def query_block(b):
        def body(j, carry):
            columns = pl.ds(pl.multiple_of(j * tile, tile), tile)
            left = factors[b, :, :, columns].reshape(2 * rank, tile)
            update = lax.dot_general(
                jnp.concatenate([left, left], axis=0),
                up_cat[...],
                (((0,), (0,)), ((), ())),
                preferred_element_type=F32,
            )
            rows = pl.ds(pl.multiple_of(b * width + j * tile, tile), tile)
            merged = (base_v[rows, :].astype(F32) + update).astype(BF16)
            q_acc[...] += jnp.dot(normed[b, :, columns], merged, preferred_element_type=F32)
            return carry

        lax.fori_loop(0, width // tile, body, 0)

    passed = []
    crossed = []
    for d in order:
        sent_factors[d].wait_recv()
        slot = factors.at[sources[d], quarter]
        crossed.append(to_dp(10 + 3 * d, across, slot, slot))
        passed.append(to_dp(11 + 3 * d, mate, slot, slot))
    query_block(t)
    for d in order:
        crossed[d].wait_recv()
        slot = factors.at[sources[d], beside]
        passed.append(to_dp(12 + 3 * d, mate, slot, slot))
    for d in order:
        passed[d].wait_recv()
        passed[shards_z - 1 + d].wait_recv()
        query_block(sources[d])

    steps = steps_rows // rows_each
    group = q_acc.shape[1] // HEAD_SIZE
    rounded = q_acc[...].astype(BF16).astype(F32)
    for s in range(steps):
        for g in range(group):
            q_rows[:, s * group + g, :] = rounded[
                s * rows_each : (s + 1) * rows_each, g * HEAD_SIZE : (g + 1) * HEAD_SIZE
            ]
    for copy in sent_kv:
        copy.wait_recv()
    new_kv = kv_send[t]
    for d in order:
        new_kv = new_kv + kv_recv[sources[d]]
    new_kv = new_kv.astype(BF16)
    new_keys = new_kv[:, :HEAD_SIZE]
    new_values = new_kv[:, HEAD_SIZE:]
    load_keys.wait()
    load_values.wait()
    load_ow.wait()
    scale = HEAD_SIZE ** (-0.5)
    pairs = steps * group
    flat_part = rows_part * pairs
    steps_part = steps * rows_part
    sent_out = []
    results = []

    def project(p):
        columns = pl.ds(pl.multiple_of(p * width, 128), width)
        return jnp.dot(att[...].astype(BF16), ow_v[:, columns], preferred_element_type=F32)

    for part in range(parts_of_rows):
        for copy in sent_caches[part]:
            copy.wait_recv()
        cut = slice(part * rows_part, (part + 1) * rows_part)
        queries = q_rows[cut].astype(BF16)
        keys = jnp.concatenate([keys_v[b, cut] for b in range(shards_z)], axis=1)
        values = jnp.concatenate([values_v[b, cut] for b in range(shards_z)], axis=1)
        old = (
            lax.dot_general(
                queries, keys, (((2,), (2,)), ((0,), (0,))), preferred_element_type=F32
            )
            * scale
        )
        fresh = (
            lax.dot_general(
                queries.reshape(flat_part, HEAD_SIZE),
                new_keys,
                (((1,), (1,)), ((), ())),
                preferred_element_type=F32,
            )
            * scale
        ).reshape(rows_part, pairs, steps_rows)
        place = lax.broadcasted_iota(jnp.int32, old.shape, 2)
        filled = [
            jnp.full((1, 1, old.shape[2]), lengths_ref[part * rows_part + r], jnp.int32)
            for r in range(rows_part)
        ]
        seen_old = place < jnp.concatenate(filled, axis=0)
        column = lax.broadcasted_iota(jnp.int32, fresh.shape, 2)
        row = lax.broadcasted_iota(jnp.int32, fresh.shape, 0) + part * rows_part
        step = lax.broadcasted_iota(jnp.int32, fresh.shape, 1) // group
        seen_new = (column % rows_each == row) & (column // rows_each <= step)
        old = jnp.where(seen_old, old, -1e30)
        fresh = jnp.where(seen_new, fresh, -1e30)
        peak = jnp.maximum(
            jnp.max(old, axis=-1, keepdims=True), jnp.max(fresh, axis=-1, keepdims=True)
        )
        old = jnp.where(seen_old, jnp.exp(old - peak), 0.0)
        fresh = jnp.where(seen_new, jnp.exp(fresh - peak), 0.0)
        total = jnp.sum(old, axis=-1, keepdims=True) + jnp.sum(fresh, axis=-1, keepdims=True)
        blended = lax.dot_general(
            old.astype(BF16), values, (((2,), (1,)), ((0,), (0,))), preferred_element_type=F32
        )
        blended = blended + jnp.dot(
            fresh.reshape(flat_part, steps_rows).astype(BF16),
            new_values,
            preferred_element_type=F32,
        ).reshape(rows_part, pairs, HEAD_SIZE)
        blend_rows[...] = blended / total
        for s in range(steps):
            for g in range(group):
                att[
                    s * rows_part : (s + 1) * rows_part, g * HEAD_SIZE : (g + 1) * HEAD_SIZE
                ] = blend_rows[:, s * group + g, :]
        for d in order:
            out_send[part, d] = project(peers[d]).astype(BF16)
            sent_out.append(
                to_z(6 + part, d, out_send.at[part, d], out_recv.at[part, d])
            )
        results.append(project(t))
    for part in range(parts_of_rows):
        result = results[part]
        for d in order:
            sent_out[part * (shards_z - 1) + d].wait_recv()
            result = result + out_recv[part, d].astype(F32)
        for s in range(steps):
            at = s * rows_each + part * rows_part
            out_wide[at : at + rows_part, :] = result[s * rows_part : (s + 1) * rows_part, :]
    out_final[...] = out_wide[...].astype(BF16)
    last = pltpu.make_async_copy(out_final, layer_out, store_sem.at[6])
    last.start()
    for k in range(1, shards_z):
        hop_finish(k)
    for copy in g1 + g2 + gs + gm + passed + crossed + sent_factors + sent_kv + sent_out:
        copy.wait_send()
    for copies in sent_caches:
        for copy in copies:
            copy.wait_send()
    for copy in stores:
        copy.wait()
    last.wait()


def write_kernel(count, *refs):
    sources, targets, held = (refs[i * count : (i + 1) * count] for i in range(3))
    sem = refs[-1]
    reads = [pltpu.make_async_copy(sources[i], held[i], sem.at[0, i]) for i in range(count)]
    writes = [pltpu.make_async_copy(held[i], targets[i], sem.at[1, i]) for i in range(count)]
    for copy in reads:
        copy.start()
    for read, write in zip(reads, writes):
        read.wait()
        write.start()
    for copy in writes:
        copy.wait()


def fused_shards(
    layer_input_states,
    base_query_weight,
    key_value_weight,
    output_weight,
    stored_keys,
    stored_values,
    lengths,
    adapter_down,
    down_first_moment,
    down_second_moment,
    down_gradients,
    adapter_up,
    up_first_moment,
    up_second_moment,
    up_gradients,
):
    z = lax.axis_size("tensor")
    steps, rows, width = layer_input_states.shape
    rank = adapter_down.shape[0]
    columns = base_query_weight.shape[1]
    group = columns // HEAD_SIZE
    flat = steps * rows
    context = stored_keys.shape[2]
    place = jax.ShapeDtypeStruct
    down = adapter_down.shape
    up = adapter_up.shape
    down_half = (rank // 2, down[1])
    up_half = (rank // 2, up[1])
    whole = pl.BlockSpec(memory_space=pl.ANY)
    in_specs = [whole] * 6 + [pl.BlockSpec(memory_space=pltpu.SMEM)] + [whole] * 8
    vm = pltpu.VMEM
    dma = pltpu.SemaphoreType.DMA
    results = pl.pallas_call(
        functools.partial(fused_kernel, z),
        out_shape=[place(down, F32)] * 3 + [place(up, F32)] * 3 + [place((flat, width), BF16)],
        in_specs=in_specs,
        out_specs=[whole] * 7,
        scratch_shapes=[
            vm((z, flat, width), BF16),
            vm((z, flat, width), BF16),
            vm(base_query_weight.shape, BF16),
            vm(key_value_weight.shape, BF16),
            vm(output_weight.shape, BF16),
            vm((z, rows, context, HEAD_SIZE), BF16),
            vm((z, rows, context, HEAD_SIZE), BF16),
            vm(down, F32),
            vm(down, F32),
            vm(down, F32),
            vm(up, F32),
            vm(up, F32),
            vm(up, F32),
            vm(down, F32),
            vm(up, F32),
            vm(down_half, BF16),
            vm(up_half, BF16),
            vm(down_half, BF16),
            vm(up_half, BF16),
            vm(down_half, BF16),
            vm(up_half, BF16),
            vm(down_half, F32),
            vm(up_half, F32),
            vm((rank // 4, down[1]), BF16),
            vm((rank // 4, up[1]), BF16),
            vm(down, BF16),
            vm(up, BF16),
            vm((z, 4, rank // 2, width), BF16),
            vm((4 * rank, columns), BF16),
            vm((z, flat, 2 * HEAD_SIZE), F32),
            vm((z, flat, 2 * HEAD_SIZE), F32),
            vm((flat, columns), F32),
            vm((rows, steps * group, HEAD_SIZE), F32),
            vm((rows // 2, steps * group, HEAD_SIZE), F32),
            vm((flat // 2, columns), F32),
            vm((2, z - 1, flat // 2, width), BF16),
            vm((2, z - 1, flat // 2, width), BF16),
            vm((flat, width), F32),
            vm((flat, width), BF16),
            dma((14,)),
            dma((7,)),
            dma((8, z - 1)),
            dma((8, z - 1)),
            dma((10 + 3 * (z - 1),)),
            dma((10 + 3 * (z - 1),)),
            dma((2, z - 1)),
            dma((2, z - 1)),
        ],
        compiler_params=pltpu.CompilerParams(
            collective_id=0, has_side_effects=True, vmem_limit_bytes=56 * 1024 * 1024
        ),
    )(
        layer_input_states.reshape(flat, width),
        base_query_weight,
        key_value_weight,
        output_weight,
        stored_keys,
        stored_values,
        lengths,
        adapter_down,
        down_first_moment,
        down_second_moment,
        down_gradients[0],
        adapter_up,
        up_first_moment,
        up_second_moment,
        up_gradients[0],
    )
    results = pl.pallas_call(
        functools.partial(write_kernel, 7),
        out_shape=[place(r.shape, r.dtype) for r in results],
        in_specs=[whole] * 7,
        out_specs=[whole] * 7,
        scratch_shapes=[vm(r.shape, r.dtype) for r in results] + [dma((2, 7))],
        compiler_params=pltpu.CompilerParams(vmem_limit_bytes=56 * 1024 * 1024),
    )(*results)
    return (*results[:6], results[6].reshape(steps, rows, width))


def solution(mesh):
    local_heads = KEY_VALUE_HEADS == mesh.shape["tensor"] and mesh.shape["dp"] == 4
    shards = fused_shards if local_heads else general_shards
    in_specs = (
        P(None, ("parts", "dp"), "tensor"),
        P(None, "tensor"),
        P("tensor", None),
        P("tensor", None),
        P(None, ("parts", "dp"), "tensor", None),
        P(None, ("parts", "dp"), "tensor", None),
        P(("parts", "dp")),
        P(None, ("parts", "tensor")),
        P(None, ("parts", "tensor")),
        P(None, ("parts", "tensor")),
        P("dp", None, ("parts", "tensor")),
        P(None, ("parts", "tensor")),
        P(None, ("parts", "tensor")),
        P(None, ("parts", "tensor")),
        P("dp", None, ("parts", "tensor")),
    )
    out_specs = (
        P(None, ("parts", "tensor")),
        P(None, ("parts", "tensor")),
        P(None, ("parts", "tensor")),
        P(None, ("parts", "tensor")),
        P(None, ("parts", "tensor")),
        P(None, ("parts", "tensor")),
        P(None, ("parts", "dp"), "tensor"),
    )
    return jax.shard_map(shards, mesh=mesh, in_specs=in_specs, out_specs=out_specs, check_vma=False)
```

```python
import functools

import jax
import jax.numpy as jnp
from jax import lax
from jax.experimental import pallas as pl
from jax.experimental.pallas import tpu as pltpu
from jax.sharding import PartitionSpec as P

QUERY_HEAD_COUNT = 32
KEY_VALUE_HEADS = 4
HEAD_SIZE = 128


beta_one = 0.9
beta_two = 0.999
learn_rate = 0.01
adam_eps = 1e-08
bias_one = 1.0 - (0.9**50) ** 2
bias_two = 1.0 - (0.999**50) ** 2
adapter_scale = 2.0
norm_eps = 1e-06


def moment_optimizer_update(param, moment, second_moment, grad):
    moment_new = beta_one * moment + (1.0 - beta_one) * grad
    second_new = beta_two * second_moment + (1.0 - beta_two) * grad * grad
    step_size = moment_new / bias_one / (jnp.sqrt(second_new / bias_two) + adam_eps)
    return (param - learn_rate * step_size, moment_new, second_new)


def general_shards(
    layer_input_states,
    base_query_weight,
    key_value_weight,
    output_weight,
    stored_keys,
    stored_values,
    lengths,
    adapter_down,
    down_first_moment,
    down_second_moment,
    down_gradients,
    adapter_up,
    up_first_moment,
    up_second_moment,
    up_gradients,
):
    tensor_count = lax.axis_size("tensor")
    tensor_rank = lax.axis_index("tensor")
    summed_down_gradient, summed_up_gradient = lax.psum((down_gradients[0], up_gradients[0]), "dp")
    adapter_down_next, down_first_moment_next, down_second_moment_next = moment_optimizer_update(
        adapter_down, down_first_moment, down_second_moment, summed_down_gradient
    )
    adapter_up_next, up_first_moment_next, up_second_moment_next = moment_optimizer_update(
        adapter_up, up_first_moment, up_second_moment, summed_up_gradient
    )
    plain_query_rows = base_query_weight.astype(jnp.float32)
    factor_update = lax.dot_general(
        lax.all_gather(adapter_down_next, "tensor", axis=1, tiled=True),
        adapter_up_next,
        (((0,), (0,)), ((), ())),
        precision=lax.Precision.HIGHEST,
        preferred_element_type=jnp.float32,
    )
    merged_query_weight = (plain_query_rows + adapter_scale * factor_update).astype(jnp.bfloat16)
    heads_local = QUERY_HEAD_COUNT // tensor_count
    local_ctx = stored_keys.shape[2]
    slot_index = tensor_rank * local_ctx + jnp.arange(local_ctx, dtype=jnp.int32)
    score_scale = HEAD_SIZE ** (-0.5)
    key_cache = stored_keys
    value_cache = stored_values
    pieces = []
    for step_index in range(layer_input_states.shape[0]):
        hidden_block = layer_input_states[step_index : step_index + 1]
        decode_key_cache = key_cache
        decode_value_cache = value_cache
        optimizer_step_count = hidden_block.shape[0]
        decode_row_count = hidden_block.shape[1]
        gathered = lax.all_gather(hidden_block, "tensor", axis=2, tiled=True)
        widened = gathered.astype(jnp.float32)
        inverse = lax.rsqrt(jnp.mean(widened * widened, axis=-1, keepdims=True) + norm_eps)
        normed = (widened * inverse).astype(jnp.bfloat16)
        normed_local = (hidden_block.astype(jnp.float32) * inverse).astype(jnp.bfloat16)
        partial_kv = jnp.einsum(
            "srd,de->sre", normed_local, key_value_weight, preferred_element_type=jnp.float32
        )
        key_value_rows = lax.psum(partial_kv, "tensor").astype(jnp.bfloat16)
        key_value_rows = key_value_rows.reshape(
            optimizer_step_count, decode_row_count, 2, KEY_VALUE_HEADS, HEAD_SIZE
        )
        queries_local = jnp.einsum(
            "srd,de->sre", normed, merged_query_weight, preferred_element_type=jnp.float32
        ).astype(jnp.bfloat16)
        query_rows = lax.all_gather(queries_local, "tensor", axis=2, tiled=True)
        query_rows = query_rows.reshape(
            optimizer_step_count,
            decode_row_count,
            KEY_VALUE_HEADS,
            QUERY_HEAD_COUNT // KEY_VALUE_HEADS,
            HEAD_SIZE,
        )
        written = (slot_index[None, :] == lengths[:, None] + step_index + 0)[None, :, :, None]
        new_keys = jnp.transpose(key_value_rows[0, :, 0], (1, 0, 2))[:, :, None, :]
        new_values = jnp.transpose(key_value_rows[0, :, 1], (1, 0, 2))[:, :, None, :]
        decode_key_cache = jnp.where(written, new_keys, decode_key_cache)
        decode_value_cache = jnp.where(written, new_values, decode_value_cache)
        step_offsets = step_index + 1 + jnp.arange(optimizer_step_count, dtype=jnp.int32)
        visible = slot_index[None, None, :] < lengths[None, :, None] + step_offsets[:, None, None]
        visible = visible[:, None, None, :, :]
        scores = (
            jnp.einsum(
                "srhgd,hrcd->shgrc",
                query_rows,
                decode_key_cache,
                preferred_element_type=jnp.float32,
            )
            * score_scale
        )
        scores = jnp.where(visible, scores, -1e30)
        row_max = jnp.max(scores, axis=-1)
        weights = jnp.where(visible, jnp.exp(scores - row_max[..., None]), 0.0)
        totals = jnp.sum(weights, axis=-1)
        blended = jnp.einsum(
            "shgrc,hrcd->shgrd",
            weights.astype(jnp.bfloat16),
            decode_value_cache,
            preferred_element_type=jnp.float32,
        )
        blended = blended.reshape(
            optimizer_step_count, tensor_count, heads_local, decode_row_count, HEAD_SIZE
        )
        row_max = row_max.reshape(optimizer_step_count, tensor_count, heads_local, decode_row_count)
        totals = totals.reshape(optimizer_step_count, tensor_count, heads_local, decode_row_count)
        blended_in = lax.all_to_all(blended, "tensor", split_axis=1, concat_axis=1, tiled=True)
        peak_scores = lax.all_to_all(row_max, "tensor", split_axis=1, concat_axis=1, tiled=True)
        masses = lax.all_to_all(totals, "tensor", split_axis=1, concat_axis=1, tiled=True)
        overall = jnp.max(peak_scores, axis=1, keepdims=True)
        factor = jnp.exp(peak_scores - overall)
        denominator = jnp.sum(factor * masses, axis=1)
        combined = jnp.sum(factor[..., None] * blended_in, axis=1) / denominator[..., None]
        combined = jnp.transpose(combined, (0, 2, 1, 3))
        attended = combined.reshape(
            combined.shape[0], combined.shape[1], heads_local * HEAD_SIZE
        ).astype(jnp.bfloat16)
        projected = jnp.einsum(
            "sre,ed->srd", attended, output_weight, preferred_element_type=jnp.float32
        )
        reduced = lax.psum_scatter(projected, "tensor", scatter_dimension=2, tiled=True)
        step_out = reduced.astype(jnp.bfloat16)
        key_cache = decode_key_cache
        value_cache = decode_value_cache
        pieces.append(step_out)
    layer_out = jnp.concatenate(pieces, axis=0)
    return (
        adapter_down_next,
        down_first_moment_next,
        down_second_moment_next,
        adapter_up_next,
        up_first_moment_next,
        up_second_moment_next,
        layer_out,
    )


MESH = pl.DeviceIdType.MESH
F32 = jnp.float32
BF16 = jnp.bfloat16


def split_high_low(value):
    high = value.astype(BF16)
    return high, (value - high.astype(F32)).astype(BF16)


def fused_kernel(
    shards_z,
    x_in,
    base_in,
    kvw_in,
    ow_in,
    keys_in,
    values_in,
    lengths_ref,
    pd_in,
    md_in,
    vd_in,
    gd_in,
    pu_in,
    mu_in,
    vu_in,
    gu_in,
    pd_out,
    md_out,
    vd_out,
    pu_out,
    mu_out,
    vu_out,
    layer_out,
    xg,
    normed,
    base_v,
    kvw_v,
    ow_v,
    keys_v,
    values_v,
    pd,
    md,
    vd,
    pu,
    mu,
    vu,
    gd,
    gu,
    g1d,
    g1u,
    g2d,
    g2u,
    r2d,
    r2u,
    gsd,
    gsu,
    factors,
    up_cat,
    kv_send,
    kv_recv,
    q_acc,
    q_rows,
    blend_rows,
    att,
    out_send,
    out_recv,
    out_wide,
    out_final,
    load_sem,
    store_sem,
    z_send,
    z_recv,
    pair_send,
    pair_recv,
    hop_send,
    hop_recv,
):
    t = lax.axis_index("tensor")
    replica = lax.axis_index("dp")
    half = lax.rem(replica, 2)
    other = 1 - half
    mate = replica + 1 - 2 * half
    across = lax.rem(replica + 2, 4)
    rank = pd.shape[0]
    hr = rank // 2
    qr = rank // 4
    side = replica // 2
    quarter = half * 2 + side
    beside = half * 2 + 1 - side
    width = xg.shape[2]
    steps_rows = xg.shape[1]

    def quarter_rows(q):
        return pl.ds(pl.multiple_of(q * qr, qr), qr)

    mine = pl.ds(pl.multiple_of(half * hr, hr), hr)
    theirs = pl.ds(pl.multiple_of(other * hr, hr), hr)
    peers = [lax.rem(t + d, shards_z) for d in range(1, shards_z)]
    sources = [lax.rem(t + shards_z - d, shards_z) for d in range(1, shards_z)]
    order = range(shards_z - 1)

    def load(index, src, dst):
        copy = pltpu.make_async_copy(src, dst, load_sem.at[index])
        copy.start()
        return copy

    def to_z(kind, d, src, dst):
        copy = pltpu.make_async_remote_copy(
            src_ref=src,
            dst_ref=dst,
            send_sem=z_send.at[kind, d],
            recv_sem=z_recv.at[kind, d],
            device_id={"tensor": peers[d]},
            device_id_type=MESH,
        )
        copy.start()
        return copy

    def to_dp(index, target, src, dst):
        copy = pltpu.make_async_remote_copy(
            src_ref=src,
            dst_ref=dst,
            send_sem=pair_send.at[index],
            recv_sem=pair_recv.at[index],
            device_id={"dp": target},
            device_id_type=MESH,
        )
        copy.start()
        return copy

    def hop_copy(way, k, block, first):
        return pltpu.make_async_remote_copy(
            src_ref=x_in if first else xg.at[block],
            dst_ref=xg.at[block],
            send_sem=hop_send.at[way, k - 1],
            recv_sem=hop_recv.at[way, k - 1],
            device_id={"tensor": peers[0] if way == 0 else sources[0]},
            device_id_type=MESH,
        )

    def hop_sends(way, k):
        if way == 0:
            return (t < shards_z - 1) & (t >= k - 1), sources[k - 2] if k > 1 else t
        return (t > 0) & (t + k <= shards_z), peers[k - 2] if k > 1 else t

    def hop_start(k):
        for way in range(2):
            sends, block = hop_sends(way, k)

            @pl.when(sends)
            def _(way=way, block=block):
                hop_copy(way, k, block, k == 1).start()

    def hop_finish(k):
        for way in range(2):
            sends, block = hop_sends(way, k)

            @pl.when(sends)
            def _(way=way, block=block):
                hop_copy(way, k, block, k == 1).wait_send()

    def hop_arrive(k):
        for way in range(2):
            gets = t >= k if way == 0 else t + k < shards_z

            @pl.when(gets)
            def _(way=way):
                block = sources[k - 1] if way == 0 else peers[k - 1]
                hop_copy(way, k, block, False).wait_recv()

    barrier = pltpu.get_barrier_semaphore()
    for p in peers:
        pl.semaphore_signal(barrier, inc=1, device_id={"tensor": p}, device_id_type=MESH)
    for p in (mate, across):
        pl.semaphore_signal(barrier, inc=1, device_id={"dp": p}, device_id_type=MESH)
    load_gd = load(0, gd_in, gd)
    load_gu = load(1, gu_in, gu)
    adam_loads = [
        load(2 + i, a, b)
        for i, (a, b) in enumerate(
            ((pd_in, pd), (md_in, md), (vd_in, vd), (pu_in, pu), (mu_in, mu), (vu_in, vu))
        )
    ]
    load_x = load(8, x_in, xg.at[t])
    load_kvw = load(9, kvw_in, kvw_v)
    load_base = load(10, base_in, base_v)
    load_keys = load(11, keys_in.at[t], keys_v.at[t])
    load_values = load(12, values_in.at[t], values_v.at[t])
    load_ow = load(13, ow_in, ow_v)
    pl.semaphore_wait(barrier, shards_z + 1)

    g1 = [
        to_dp(0, mate, gd_in.at[theirs], g1d),
        to_dp(1, mate, gu_in.at[theirs], g1u),
    ]
    hop_start(1)

    load_gd.wait()
    load_gu.wait()
    for copy in g1:
        copy.wait_recv()
    g2d[...] = gd[mine, :] + g1d[...]
    g2u[...] = gu[mine, :] + g1u[...]
    kept = quarter_rows(side)
    given = quarter_rows(1 - side)
    g2 = [to_dp(2, across, g2d.at[given], r2d), to_dp(3, across, g2u.at[given], r2u)]
    hop_arrive(1)
    hop_start(2)
    parts_of_rows = 2
    rows_each = q_rows.shape[0]
    rows_part = rows_each // parts_of_rows

    def send_caches(part):
        cut = pl.ds(part * rows_part, rows_part)
        return [
            to_z(2 + 2 * part + i, d, source.at[peers[d], cut], held.at[t, cut])
            for d in order
            for i, (source, held) in enumerate(((keys_in, keys_v), (values_in, values_v)))
        ]

    sent_caches = [send_caches(0)]
    for copy in adam_loads:
        copy.wait()
    for copy in g2:
        copy.wait_recv()
    own = quarter_rows(quarter)
    next_to = quarter_rows(beside)
    gsd[own, :] = g2d[kept, :] + r2d[...]
    gsu[own, :] = g2u[kept, :] + r2u[...]
    gs = [
        to_dp(4, across, gsd.at[own], gsd.at[own]),
        to_dp(5, across, gsu.at[own], gsu.at[own]),
    ]
    gm = [
        to_dp(6, mate, gsd.at[own], gsd.at[own]),
        to_dp(7, mate, gsu.at[own], gsu.at[own]),
    ]

    def step_down(q):
        rows = quarter_rows(q)
        new = moment_optimizer_update(pd[rows, :], md[rows, :], vd[rows, :], gsd[rows, :])
        pd[rows, :], md[rows, :], vd[rows, :] = new
        high, low = split_high_low(new[0])
        factors[t, q, 0:qr, :] = high
        factors[t, q, qr : 2 * qr, :] = low

    step_down(quarter)
    sent_factors = [to_z(0, d, factors.at[t, quarter], factors.at[t, quarter]) for d in order]
    hop_arrive(2)
    hop_start(3)
    for copy in gs:
        copy.wait_recv()
    gm += [
        to_dp(8, mate, gsd.at[next_to], gsd.at[next_to]),
        to_dp(9, mate, gsu.at[next_to], gsu.at[next_to]),
    ]
    step_down(beside)
    for copy in gm:
        copy.wait_recv()
    step_down(other * 2)
    step_down(other * 2 + 1)
    new_up = moment_optimizer_update(pu[...], mu[...], vu[...], gsu[...])
    pu[...], mu[...], vu[...] = new_up
    stores = []
    for i, (a, b) in enumerate(
        ((pd, pd_out), (md, md_out), (vd, vd_out), (pu, pu_out), (mu, mu_out), (vu, vu_out))
    ):
        copy = pltpu.make_async_copy(a, b, store_sem.at[i])
        copy.start()
        stores.append(copy)
    up_parts = split_high_low(adapter_scale * new_up[0])
    for i in range(2):
        for j in range(4):
            piece = up_parts[i][j * qr : (j + 1) * qr, :]
            at = (i * 4 + j) * 2 * qr
            up_cat[at : at + qr, :] = piece
            up_cat[at + qr : at + 2 * qr, :] = piece

    load_x.wait()
    hop_arrive(3)
    squares = jnp.zeros((steps_rows, 1), F32)
    for b in range(shards_z):
        wide = xg[b].astype(F32)
        squares = squares + jnp.sum(wide * wide, axis=-1, keepdims=True)
    inverse = lax.rsqrt(squares / (width * shards_z) + norm_eps)
    for b in range(shards_z):
        normed[b] = (xg[b].astype(F32) * inverse).astype(BF16)
    load_kvw.wait()
    local_rows = normed[t]
    kv_half = KEY_VALUE_HEADS * HEAD_SIZE
    for p in range(shards_z):
        for kind in range(2):
            at = kind * kv_half + p * HEAD_SIZE
            kv_send[p, :, kind * HEAD_SIZE : (kind + 1) * HEAD_SIZE] = jnp.dot(
                local_rows, kvw_v[:, at : at + HEAD_SIZE], preferred_element_type=F32
            )
    sent_kv = [to_z(1, d, kv_send.at[peers[d]], kv_recv.at[t]) for d in order]

    load_base.wait()
    q_acc[...] = jnp.zeros_like(q_acc)
    tile = 256

    def query_block(b):
        def body(j, carry):
            columns = pl.ds(pl.multiple_of(j * tile, tile), tile)
            left = factors[b, :, :, columns].reshape(2 * rank, tile)
            update = lax.dot_general(
                jnp.concatenate([left, left], axis=0),
                up_cat[...],
                (((0,), (0,)), ((), ())),
                preferred_element_type=F32,
            )
            rows = pl.ds(pl.multiple_of(b * width + j * tile, tile), tile)
            merged = (base_v[rows, :].astype(F32) + update).astype(BF16)
            q_acc[...] += jnp.dot(normed[b, :, columns], merged, preferred_element_type=F32)
            return carry

        lax.fori_loop(0, width // tile, body, 0)

    passed = []
    crossed = []
    for d in order:
        sent_factors[d].wait_recv()
        slot = factors.at[sources[d], quarter]
        crossed.append(to_dp(10 + 3 * d, across, slot, slot))
        passed.append(to_dp(11 + 3 * d, mate, slot, slot))
    sent_caches.append(send_caches(1))
    query_block(t)
    for d in order:
        crossed[d].wait_recv()
        slot = factors.at[sources[d], beside]
        passed.append(to_dp(12 + 3 * d, mate, slot, slot))
    for d in order:
        passed[d].wait_recv()
        passed[shards_z - 1 + d].wait_recv()
        query_block(sources[d])

    steps = steps_rows // rows_each
    group = q_acc.shape[1] // HEAD_SIZE
    rounded = q_acc[...].astype(BF16).astype(F32)
    for s in range(steps):
        for g in range(group):
            q_rows[:, s * group + g, :] = rounded[
                s * rows_each : (s + 1) * rows_each, g * HEAD_SIZE : (g + 1) * HEAD_SIZE
            ]
    for copy in sent_kv:
        copy.wait_recv()
    new_kv = kv_send[t]
    for d in order:
        new_kv = new_kv + kv_recv[sources[d]]
    new_kv = new_kv.astype(BF16)
    new_keys = new_kv[:, :HEAD_SIZE]
    new_values = new_kv[:, HEAD_SIZE:]
    load_keys.wait()
    load_values.wait()
    load_ow.wait()
    scale = HEAD_SIZE ** (-0.5)
    pairs = steps * group
    flat_part = rows_part * pairs
    steps_part = steps * rows_part
    sent_out = []
    results = []

    def project(p):
        columns = pl.ds(pl.multiple_of(p * width, 128), width)
        return jnp.dot(att[...].astype(BF16), ow_v[:, columns], preferred_element_type=F32)

    for part in range(parts_of_rows):
        for copy in sent_caches[part]:
            copy.wait_recv()
        cut = slice(part * rows_part, (part + 1) * rows_part)
        queries = q_rows[cut].astype(BF16)
        keys = jnp.concatenate([keys_v[b, cut] for b in range(shards_z)], axis=1)
        values = jnp.concatenate([values_v[b, cut] for b in range(shards_z)], axis=1)
        old = (
            lax.dot_general(
                queries, keys, (((2,), (2,)), ((0,), (0,))), preferred_element_type=F32
            )
            * scale
        )
        fresh = (
            lax.dot_general(
                queries.reshape(flat_part, HEAD_SIZE),
                new_keys,
                (((1,), (1,)), ((), ())),
                preferred_element_type=F32,
            )
            * scale
        ).reshape(rows_part, pairs, steps_rows)
        place = lax.broadcasted_iota(jnp.int32, old.shape, 2)
        filled = [
            jnp.full((1, 1, old.shape[2]), lengths_ref[part * rows_part + r], jnp.int32)
            for r in range(rows_part)
        ]
        seen_old = place < jnp.concatenate(filled, axis=0)
        column = lax.broadcasted_iota(jnp.int32, fresh.shape, 2)
        row = lax.broadcasted_iota(jnp.int32, fresh.shape, 0) + part * rows_part
        step = lax.broadcasted_iota(jnp.int32, fresh.shape, 1) // group
        seen_new = (column % rows_each == row) & (column // rows_each <= step)
        old = jnp.where(seen_old, old, -1e30)
        fresh = jnp.where(seen_new, fresh, -1e30)
        peak = jnp.maximum(
            jnp.max(old, axis=-1, keepdims=True), jnp.max(fresh, axis=-1, keepdims=True)
        )
        old = jnp.where(seen_old, jnp.exp(old - peak), 0.0)
        fresh = jnp.where(seen_new, jnp.exp(fresh - peak), 0.0)
        total = jnp.sum(old, axis=-1, keepdims=True) + jnp.sum(fresh, axis=-1, keepdims=True)
        blended = lax.dot_general(
            old.astype(BF16), values, (((2,), (1,)), ((0,), (0,))), preferred_element_type=F32
        )
        blended = blended + jnp.dot(
            fresh.reshape(flat_part, steps_rows).astype(BF16),
            new_values,
            preferred_element_type=F32,
        ).reshape(rows_part, pairs, HEAD_SIZE)
        blend_rows[...] = blended / total
        for s in range(steps):
            for g in range(group):
                att[
                    s * rows_part : (s + 1) * rows_part, g * HEAD_SIZE : (g + 1) * HEAD_SIZE
                ] = blend_rows[:, s * group + g, :]
        for d in order:
            out_send[part, d] = project(peers[d]).astype(BF16)
            sent_out.append(
                to_z(6 + part, d, out_send.at[part, d], out_recv.at[part, d])
            )
        results.append(project(t))
    for part in range(parts_of_rows):
        result = results[part]
        for d in order:
            sent_out[part * (shards_z - 1) + d].wait_recv()
            result = result + out_recv[part, d].astype(F32)
        for s in range(steps):
            at = s * rows_each + part * rows_part
            out_wide[at : at + rows_part, :] = result[s * rows_part : (s + 1) * rows_part, :]
    out_final[...] = out_wide[...].astype(BF16)
    last = pltpu.make_async_copy(out_final, layer_out, store_sem.at[6])
    last.start()
    for k in range(1, shards_z):
        hop_finish(k)
    for copy in g1 + g2 + gs + gm + passed + crossed + sent_factors + sent_kv + sent_out:
        copy.wait_send()
    for copies in sent_caches:
        for copy in copies:
            copy.wait_send()
    for copy in stores:
        copy.wait()
    last.wait()


def write_kernel(count, *refs):
    sources, targets, held = (refs[i * count : (i + 1) * count] for i in range(3))
    sem = refs[-1]
    reads = [pltpu.make_async_copy(sources[i], held[i], sem.at[0, i]) for i in range(count)]
    writes = [pltpu.make_async_copy(held[i], targets[i], sem.at[1, i]) for i in range(count)]
    for copy in reads:
        copy.start()
    for read, write in zip(reads, writes):
        read.wait()
        write.start()
    for copy in writes:
        copy.wait()


def fused_shards(
    layer_input_states,
    base_query_weight,
    key_value_weight,
    output_weight,
    stored_keys,
    stored_values,
    lengths,
    adapter_down,
    down_first_moment,
    down_second_moment,
    down_gradients,
    adapter_up,
    up_first_moment,
    up_second_moment,
    up_gradients,
):
    z = lax.axis_size("tensor")
    steps, rows, width = layer_input_states.shape
    rank = adapter_down.shape[0]
    columns = base_query_weight.shape[1]
    group = columns // HEAD_SIZE
    flat = steps * rows
    context = stored_keys.shape[2]
    place = jax.ShapeDtypeStruct
    down = adapter_down.shape
    up = adapter_up.shape
    down_half = (rank // 2, down[1])
    up_half = (rank // 2, up[1])
    whole = pl.BlockSpec(memory_space=pl.ANY)
    in_specs = [whole] * 6 + [pl.BlockSpec(memory_space=pltpu.SMEM)] + [whole] * 8
    vm = pltpu.VMEM
    dma = pltpu.SemaphoreType.DMA
    results = pl.pallas_call(
        functools.partial(fused_kernel, z),
        out_shape=[place(down, F32)] * 3 + [place(up, F32)] * 3 + [place((flat, width), BF16)],
        in_specs=in_specs,
        out_specs=[whole] * 7,
        scratch_shapes=[
            vm((z, flat, width), BF16),
            vm((z, flat, width), BF16),
            vm(base_query_weight.shape, BF16),
            vm(key_value_weight.shape, BF16),
            vm(output_weight.shape, BF16),
            vm((z, rows, context, HEAD_SIZE), BF16),
            vm((z, rows, context, HEAD_SIZE), BF16),
            vm(down, F32),
            vm(down, F32),
            vm(down, F32),
            vm(up, F32),
            vm(up, F32),
            vm(up, F32),
            vm(down, F32),
            vm(up, F32),
            vm(down_half, F32),
            vm(up_half, F32),
            vm(down_half, F32),
            vm(up_half, F32),
            vm((rank // 4, down[1]), F32),
            vm((rank // 4, up[1]), F32),
            vm(down, F32),
            vm(up, F32),
            vm((z, 4, rank // 2, width), BF16),
            vm((4 * rank, columns), BF16),
            vm((z, flat, 2 * HEAD_SIZE), F32),
            vm((z, flat, 2 * HEAD_SIZE), F32),
            vm((flat, columns), F32),
            vm((rows, steps * group, HEAD_SIZE), F32),
            vm((rows // 2, steps * group, HEAD_SIZE), F32),
            vm((flat // 2, columns), F32),
            vm((2, z - 1, flat // 2, width), BF16),
            vm((2, z - 1, flat // 2, width), BF16),
            vm((flat, width), F32),
            vm((flat, width), BF16),
            dma((14,)),
            dma((7,)),
            dma((8, z - 1)),
            dma((8, z - 1)),
            dma((10 + 3 * (z - 1),)),
            dma((10 + 3 * (z - 1),)),
            dma((2, z - 1)),
            dma((2, z - 1)),
        ],
        compiler_params=pltpu.CompilerParams(
            collective_id=0, has_side_effects=True, vmem_limit_bytes=56 * 1024 * 1024
        ),
    )(
        layer_input_states.reshape(flat, width),
        base_query_weight,
        key_value_weight,
        output_weight,
        stored_keys,
        stored_values,
        lengths,
        adapter_down,
        down_first_moment,
        down_second_moment,
        down_gradients[0],
        adapter_up,
        up_first_moment,
        up_second_moment,
        up_gradients[0],
    )
    results = pl.pallas_call(
        functools.partial(write_kernel, 7),
        out_shape=[place(r.shape, r.dtype) for r in results],
        in_specs=[whole] * 7,
        out_specs=[whole] * 7,
        scratch_shapes=[vm(r.shape, r.dtype) for r in results] + [dma((2, 7))],
        compiler_params=pltpu.CompilerParams(vmem_limit_bytes=56 * 1024 * 1024),
    )(*results)
    return (*results[:6], results[6].reshape(steps, rows, width))


def solution(mesh):
    local_heads = KEY_VALUE_HEADS == mesh.shape["tensor"] and mesh.shape["dp"] == 4
    shards = fused_shards if local_heads else general_shards
    in_specs = (
        P(None, ("parts", "dp"), "tensor"),
        P(None, "tensor"),
        P("tensor", None),
        P("tensor", None),
        P(None, ("parts", "dp"), "tensor", None),
        P(None, ("parts", "dp"), "tensor", None),
        P(("parts", "dp")),
        P(None, ("parts", "tensor")),
        P(None, ("parts", "tensor")),
        P(None, ("parts", "tensor")),
        P("dp", None, ("parts", "tensor")),
        P(None, ("parts", "tensor")),
        P(None, ("parts", "tensor")),
        P(None, ("parts", "tensor")),
        P("dp", None, ("parts", "tensor")),
    )
    out_specs = (
        P(None, ("parts", "tensor")),
        P(None, ("parts", "tensor")),
        P(None, ("parts", "tensor")),
        P(None, ("parts", "tensor")),
        P(None, ("parts", "tensor")),
        P(None, ("parts", "tensor")),
        P(None, ("parts", "dp"), "tensor"),
    )
    return jax.shard_map(shards, mesh=mesh, in_specs=in_specs, out_specs=out_specs, check_vma=False)
```
